256 devices in a mesh: ctx: 32 (over z, x_hi, core), tp: 8 (over x_lo, y).
Axes of the slice: x: 4 (x_hi: 2, x_lo: 2; x = x_hi * 2 + x_lo), y: 4, z: 8, core: 2. Of those that a mesh axis runs over, the one named last changes fastest.
Arguments:
- layer_input_rows: bfloat16 [32768, 4608], P('ctx', 'tp'), may hold values from -6 to 6
- queries: bfloat16 [32768, 2048], P('ctx', 'tp'), may hold values from -6 to 6
- keys: bfloat16 [32768, 1024], P('ctx', 'tp'), may hold values from -6 to 6
- values: bfloat16 [32768, 1024], P('ctx', 'tp'), may hold values from -6 to 6
- output_gradient: bfloat16 [32768, 2048], P('ctx', 'tp'), may hold values from -6 to 6
- outputs: bfloat16 [32768, 2048], P('ctx', 'tp'), may hold values from -6 to 6
- softmax_log_totals: float32 [16, 32768], P('tp', 'ctx'), may hold values from 3 to 5
- token_document_index: int32 [32768], P('ctx'), may hold values from 0 to 3, never falling along the last dimension, each value on 1 to 16384 neighbouring positions
- query_adapter_down_weight: bfloat16 [4608, 128], P('tp'), may hold values from -0.09375 to 0.09375
- query_adapter_up_weight: bfloat16 [128, 2048], P(None, 'tp'), may hold values from -0.125 to 0.125
- value_adapter_down_weight: bfloat16 [4608, 128], P('tp'), may hold values from -0.09375 to 0.09375
- value_adapter_up_weight: bfloat16 [128, 1024], P(None, 'tp'), may hold values from -0.1875 to 0.1875
Outputs:
- key_grad: bfloat16 [32768, 1024], P('ctx', 'tp')
- grad_a_query: float32 [4608, 128], P('tp')
- grad_b_query: float32 [128, 2048], P(None, 'tp')
- grad_a_value: float32 [4608, 128], P('tp')
- grad_b_value: float32 [128, 1024], P(None, 'tp')
The draws below stay inside these ranges and needn't reach their ends.
Inputs may be any that keep to these rules, and one draw needn't show every extreme that they name: `token_document_index`: ids never fall along the tokens; each document holds 1 to 16384 tokens and one holds exactly 16384.
All inputs are finite; a program needn't handle non-finite values.
Results may differ from the reference program's by a relative error of at most 0.0058.
Values may be sent and summed in bfloat16 or wider, within the bound.
A program may use at most 128 MiB of HBM per device.

```python
import math
import jax
import jax.numpy as jnp
import numpy as np
from jax import lax

MODEL_WIDTH = 4608
QUERY_HEADS = 16
KEY_VALUE_HEADS = 8
HEAD_WIDTH = 128
ADAPTER_RANK = 128
WINDOW = 4096
TOK_DEV = 1024
TOKENS = 32768


def shard_levels(stream_key, extent, shards, least, high):
    loudness, own = 1.0, jax.random.fold_in(stream_key, 6)
    for position, shards_of in shards:
        steps = jnp.exp(jax.random.uniform(jax.random.fold_in(own, position), (shards_of,), jnp.float32, least / len(shards), high / len(shards)))
        loudness = loudness * jnp.repeat(steps, extent[position] // shards_of).reshape([-1 if axis == position else 1 for axis in range(len(extent))])
    return loudness


def length_profile(amount, total, reach, slope):
    weights = [(1 << 20) // math.isqrt(rank ** slope) + 1 for rank in range(2, amount + 1)]
    spare, counts = total - reach - (amount - 1), [1] * (amount - 1)
    while spare > 0:
        movable = [i for i in range(amount - 1) if counts[i] < reach]
        whole, budget = sum([weights[i] for i in movable]), spare
        for i in movable:
            extra = min(reach - counts[i], max(1, budget * weights[i] // whole), spare)
            counts[i] = counts[i] + extra
            spare = spare - extra
    return np.array([reach] + counts)


def uneven_parts(own_key, count, total, most, lean):
    if count == 2:
        one = jax.random.randint(own_key, (), max(1, total - most), min(most, total - 1) + 1)
        return jnp.stack([one, total - one])
    sizes = jnp.asarray(length_profile(count, total, most, lean), jnp.int32)
    twos = (count - 1) // 2
    source_of, taker = sizes[1:1 + 2 * twos:2], sizes[2:2 + 2 * twos:2]
    room = jnp.minimum(source_of - 1, most - taker)
    passed = jax.random.randint(jax.random.fold_in(own_key, 1), (twos,), 0, 1 << 20) % (room + 1)
    sizes = sizes.at[1:1 + 2 * twos:2].set(source_of - passed).at[2:2 + 2 * twos:2].set(taker + passed)
    return sizes[jax.random.permutation(jax.random.fold_in(own_key, 2), count)]


def centred(own_key, extent, scale, most, cuts=(), kind=jnp.bfloat16):
    entries = scale * jax.random.normal(own_key, extent, jnp.float32)
    if cuts:
        entries = entries * shard_levels(own_key, extent, cuts, -0.22, 0.18)
    return jnp.clip(entries, -most, most).astype(kind)


def setup_inputs(seed: int = 0) -> dict:
    splits = jax.random.split(jax.random.key(seed), 13)
    layer_input_rows = centred(splits[0], (TOKENS, MODEL_WIDTH), 1.0, 6.0, ((0, 32), (1, 8)))
    queries = centred(splits[1], (TOKENS, QUERY_HEADS * HEAD_WIDTH), 1.0, 6.0, ((0, 32), (1, 8)))
    keys = centred(splits[2], (TOKENS, KEY_VALUE_HEADS * HEAD_WIDTH), 1.0, 6.0, ((0, 32), (1, 8)))
    values = centred(splits[3], (TOKENS, KEY_VALUE_HEADS * HEAD_WIDTH), 1.0, 6.0, ((0, 32), (1, 8)))
    output_gradient = centred(splits[4], (TOKENS, QUERY_HEADS * HEAD_WIDTH), 1.0, 6.0, ((0, 32), (1, 8)))
    outputs = centred(splits[5], (TOKENS, QUERY_HEADS * HEAD_WIDTH), 1.0, 6.0, ((0, 32), (1, 8)))
    softmax_log_totals = jnp.clip(3.0 + 2.0 * jax.random.uniform(splits[6], (QUERY_HEADS, TOKENS), jnp.float32) ** shard_levels(splits[6], (QUERY_HEADS, TOKENS), ((0, 8), (1, 32)), -0.2, 0.2), 3.0, 5.0)
    token_document_index = jnp.searchsorted(jnp.cumsum(uneven_parts(splits[7], 4, TOKENS, TOKENS // 2, 0)), jnp.arange(TOKENS), side="right").astype(jnp.int32)
    query_adapter_down_weight = centred(splits[8], (MODEL_WIDTH, ADAPTER_RANK), MODEL_WIDTH ** -0.5, 0.09375, ((0, 8),))
    query_adapter_up_weight = centred(splits[9], (ADAPTER_RANK, QUERY_HEADS * HEAD_WIDTH), (QUERY_HEADS * HEAD_WIDTH) ** -0.5, 0.125, ((1, 8),))
    value_adapter_down_weight = centred(splits[10], (MODEL_WIDTH, ADAPTER_RANK), MODEL_WIDTH ** -0.5, 0.09375, ((0, 8),))
    value_adapter_up_weight = centred(splits[11], (ADAPTER_RANK, KEY_VALUE_HEADS * HEAD_WIDTH), (KEY_VALUE_HEADS * HEAD_WIDTH) ** -0.5, 0.1875, ((1, 8),))
    return dict(layer_input_rows=layer_input_rows, queries=queries, keys=keys, values=values, output_gradient=output_gradient, outputs=outputs, softmax_log_totals=softmax_log_totals, token_document_index=token_document_index, query_adapter_down_weight=query_adapter_down_weight, query_adapter_up_weight=query_adapter_up_weight, value_adapter_down_weight=value_adapter_down_weight, value_adapter_up_weight=value_adapter_up_weight)


SCORE_SCALE = 144.0 ** (-0.5)

def attend(query_part, grad_part, normalizer, row_delta, seg_query, pos_query, key_part, value_part, seg_key, pos_key):
    scores = jnp.einsum('ikgd,jkd->kgij', query_part, key_part) * SCORE_SCALE
    distance = pos_query[:, None] - pos_key[None, :]
    allowed = (distance >= 0) & (distance < WINDOW) & (seg_query[:, None] == seg_key[None, :])
    probs = jnp.where(allowed[None, None], jnp.exp(scores - normalizer[:, :, :, None]), 0.0)
    dprobs = jnp.einsum('ikgd,jkd->kgij', grad_part, value_part)
    dscore = probs * (dprobs - row_delta[:, :, :, None])
    probs_low = lax.optimization_barrier(probs.astype(jnp.bfloat16)).astype(jnp.float32)
    dscore_low = lax.optimization_barrier(dscore.astype(jnp.bfloat16)).astype(jnp.float32)
    return (probs_low, dscore_low)

def reference(layer_input_rows, queries, keys, values, output_gradient, outputs, softmax_log_totals, token_document_index, query_adapter_down_weight, query_adapter_up_weight, value_adapter_down_weight, value_adapter_up_weight):
    q_group = QUERY_HEADS // KEY_VALUE_HEADS
    ref_block = min(TOK_DEV, 512)
    n_blocks = TOKENS // ref_block
    query_heads = queries.astype(jnp.float32).reshape(TOKENS, KEY_VALUE_HEADS, q_group, HEAD_WIDTH)
    grad_heads = output_gradient.astype(jnp.float32).reshape(TOKENS, KEY_VALUE_HEADS, q_group, HEAD_WIDTH)
    out_heads = outputs.astype(jnp.float32).reshape(TOKENS, KEY_VALUE_HEADS, q_group, HEAD_WIDTH)
    key_heads = keys.astype(jnp.float32).reshape(TOKENS, KEY_VALUE_HEADS, HEAD_WIDTH)
    value_heads = values.astype(jnp.float32).reshape(TOKENS, KEY_VALUE_HEADS, HEAD_WIDTH)
    row_delta = lax.optimization_barrier(jnp.sum(grad_heads * out_heads, axis=3)).transpose(1, 2, 0)
    normalizer = softmax_log_totals.reshape(KEY_VALUE_HEADS, q_group, TOKENS)
    positions = jnp.arange(TOKENS, dtype=jnp.int32)
    key_pad = jnp.concatenate([jnp.zeros((WINDOW, KEY_VALUE_HEADS, HEAD_WIDTH), key_heads.dtype), key_heads], axis=0)
    value_pad = jnp.concatenate([jnp.zeros((WINDOW, KEY_VALUE_HEADS, HEAD_WIDTH), value_heads.dtype), value_heads], axis=0)
    seg_key_pad = jnp.concatenate([jnp.full((WINDOW,), -1, jnp.int32), token_document_index.astype(jnp.int32)])
    pos_key_pad = jnp.arange(-WINDOW, TOKENS, dtype=jnp.int32)

    def query_block(index):
        start = (index * ref_block).astype(jnp.int32)
        query_part = lax.dynamic_slice_in_dim(query_heads, start, ref_block, 0)
        grad_part = lax.dynamic_slice_in_dim(grad_heads, start, ref_block, 0)
        norm_part = lax.dynamic_slice_in_dim(normalizer, start, ref_block, 2)
        delta_part = lax.dynamic_slice_in_dim(row_delta, start, ref_block, 2)
        seg_part = lax.dynamic_slice_in_dim(token_document_index, start, ref_block, 0)
        pos_part = lax.dynamic_slice_in_dim(positions, start, ref_block, 0)
        key_part = lax.dynamic_slice_in_dim(key_pad, start, WINDOW + ref_block, 0)
        value_part = lax.dynamic_slice_in_dim(value_pad, start, WINDOW + ref_block, 0)
        seg_keys = lax.dynamic_slice_in_dim(seg_key_pad, start, WINDOW + ref_block, 0)
        pos_keys = lax.dynamic_slice_in_dim(pos_key_pad, start, WINDOW + ref_block, 0)
        probs_low, dscore_low = attend(query_part, grad_part, norm_part, delta_part, seg_part, pos_part, key_part, value_part, seg_keys, pos_keys)
        result = SCORE_SCALE * jnp.einsum('kgij,jkd->ikgd', dscore_low, key_part)
        return result.reshape(ref_block, QUERY_HEADS * HEAD_WIDTH)
    query_gradient_rows = lax.map(query_block, jnp.arange(n_blocks, dtype=jnp.int32))
    query_gradient_rows = query_gradient_rows.reshape(TOKENS, QUERY_HEADS * HEAD_WIDTH).astype(jnp.bfloat16)
    query_pad = jnp.concatenate([query_heads, jnp.zeros((WINDOW, KEY_VALUE_HEADS, q_group, HEAD_WIDTH), query_heads.dtype)], axis=0)
    grad_pad = jnp.concatenate([grad_heads, jnp.zeros((WINDOW, KEY_VALUE_HEADS, q_group, HEAD_WIDTH), grad_heads.dtype)], axis=0)
    norm_pad = jnp.concatenate([normalizer, jnp.zeros((KEY_VALUE_HEADS, q_group, WINDOW), normalizer.dtype)], axis=2)
    delta_pad = jnp.concatenate([row_delta, jnp.zeros((KEY_VALUE_HEADS, q_group, WINDOW), row_delta.dtype)], axis=2)
    seg_query_pad = jnp.concatenate([token_document_index.astype(jnp.int32), jnp.full((WINDOW,), -2, jnp.int32)])
    pos_query_pad = jnp.arange(0, TOKENS + WINDOW, dtype=jnp.int32)

    def key_block(index):
        start = (index * ref_block).astype(jnp.int32)
        key_part = lax.dynamic_slice_in_dim(key_heads, start, ref_block, 0)
        value_part = lax.dynamic_slice_in_dim(value_heads, start, ref_block, 0)
        seg_keys = lax.dynamic_slice_in_dim(token_document_index, start, ref_block, 0)
        pos_keys = lax.dynamic_slice_in_dim(positions, start, ref_block, 0)
        query_part = lax.dynamic_slice_in_dim(query_pad, start, WINDOW + ref_block, 0)
        grad_part = lax.dynamic_slice_in_dim(grad_pad, start, WINDOW + ref_block, 0)
        norm_part = lax.dynamic_slice_in_dim(norm_pad, start, WINDOW + ref_block, 2)
        delta_part = lax.dynamic_slice_in_dim(delta_pad, start, WINDOW + ref_block, 2)
        seg_part = lax.dynamic_slice_in_dim(seg_query_pad, start, WINDOW + ref_block, 0)
        pos_part = lax.dynamic_slice_in_dim(pos_query_pad, start, WINDOW + ref_block, 0)
        probs_low, dscore_low = attend(query_part, grad_part, norm_part, delta_part, seg_part, pos_part, key_part, value_part, seg_keys, pos_keys)
        key_result = SCORE_SCALE * jnp.einsum('kgij,ikgd->jkd', dscore_low, query_part)
        value_result = jnp.einsum('kgij,ikgd->jkd', probs_low, grad_part)
        return (key_result.reshape(ref_block, KEY_VALUE_HEADS * HEAD_WIDTH), value_result.reshape(ref_block, KEY_VALUE_HEADS * HEAD_WIDTH))
    key_grad, value_gradient_rows = lax.map(key_block, jnp.arange(n_blocks, dtype=jnp.int32))
    key_grad = key_grad.reshape(TOKENS, KEY_VALUE_HEADS * HEAD_WIDTH).astype(jnp.bfloat16)
    value_gradient_rows = value_gradient_rows.reshape(TOKENS, KEY_VALUE_HEADS * HEAD_WIDTH).astype(jnp.bfloat16)
    token_scale = 1.0 / math.sqrt(TOKENS)
    query_adapter_input = jnp.dot(layer_input_rows, query_adapter_down_weight, preferred_element_type=jnp.float32).astype(jnp.bfloat16)
    value_adapter_input = jnp.dot(layer_input_rows, value_adapter_down_weight, preferred_element_type=jnp.float32).astype(jnp.bfloat16)
    query_backward_rows = jnp.dot(query_gradient_rows, query_adapter_up_weight.T, preferred_element_type=jnp.float32).astype(jnp.bfloat16)
    value_backward_rows = jnp.dot(value_gradient_rows, value_adapter_up_weight.T, preferred_element_type=jnp.float32).astype(jnp.bfloat16)
    grad_a_query = jnp.dot(layer_input_rows.T, query_backward_rows, preferred_element_type=jnp.float32) * token_scale
    grad_b_query = jnp.dot(query_adapter_input.T, query_gradient_rows, preferred_element_type=jnp.float32) * token_scale
    grad_a_value = jnp.dot(layer_input_rows.T, value_backward_rows, preferred_element_type=jnp.float32) * token_scale
    grad_b_value = jnp.dot(value_adapter_input.T, value_gradient_rows, preferred_element_type=jnp.float32) * token_scale
    return (key_grad, grad_a_query, grad_b_query, grad_a_value, grad_b_value)
```

```python
import functools
import math

import jax
import jax.numpy as jnp
from jax import lax
from jax.experimental import pallas as pl
from jax.experimental.pallas import tpu as pltpu
from jax.sharding import PartitionSpec as P

HEAD = 128
HEADS_LOCAL = 2
REACH = 4
SCORE_SCALE = 144.0 ** (-0.5)
LOG2E = 1.4426950408889634
BF16 = jnp.bfloat16
F32 = jnp.float32
MESH = pl.DeviceIdType.MESH


def contract(a, b, dim_a, dim_b):
    return lax.dot_general(
        a, b, (((dim_a,), (dim_b,)), ((), ())), preferred_element_type=F32
    )


def kernel(
    n_ctx,
    n_tp,
    x_ref,
    q_ref,
    k_ref,
    v_ref,
    do_ref,
    o_ref,
    lse_ref,
    seg_ref,
    aq_ref,
    bq_ref,
    av_ref,
    bv_ref,
    key_grad_ref,
    ga_q_ref,
    gb_q_ref,
    ga_v_ref,
    gb_v_ref,
    k_in,
    v_in,
    seg_in,
    q_st,
    do_st,
    lse_st,
    delta_st,
    thr_st,
    dk_acc,
    dv_acc,
    dk_own,
    dv_own,
    dq_acc,
    dq_low,
    dv_low,
    part_out,
    part_in,
    low_s,
    low_r,
    low_g,
    back_s,
    back_r,
    back_g,
    g_all,
    half_s,
    half_r,
    piece_s,
    piece_r,
    g_out,
    kv_send,
    kv_recv,
    part_send,
    part_recv,
    tp_send,
    tp_recv,
    half_send,
    half_recv,
    piece_send,
    piece_recv,
):
    rows = k_ref.shape[0]
    width = x_ref.shape[1]
    chunk = rows // n_tp
    pairs = n_ctx // 2
    total = g_all.shape[0]
    half = total // 2
    piece = half // pairs
    c = lax.axis_index("ctx")
    t = lax.axis_index("tp")
    core = lax.rem(c, 2)
    pair = c // 2

    def ctx_at(offset):
        return lax.rem(c + (offset + n_ctx), n_ctx)

    def tp_at(offset):
        return lax.rem(t + offset, n_tp)

    barrier = pltpu.get_barrier_semaphore()
    offsets = {s % n_ctx for s in range(-REACH, REACH + 1)} | set(range(0, n_ctx, 2))
    offsets = sorted(offsets - {0})
    for offset in offsets:
        pl.semaphore_signal(
            barrier, inc=1, device_id={"ctx": ctx_at(offset)}, device_id_type=MESH
        )
    for offset in range(1, n_tp):
        pl.semaphore_signal(
            barrier, inc=1, device_id={"tp": tp_at(offset)}, device_id_type=MESH
        )
    pl.semaphore_wait(barrier, len(offsets) + n_tp - 1)

    def kv_copies(step):
        found = []
        for which, (src, dst) in enumerate(
            ((k_ref, k_in), (v_ref, v_in), (seg_ref, seg_in))
        ):
            found.append(
                pltpu.make_async_remote_copy(
                    src_ref=src,
                    dst_ref=dst.at[step - 1],
                    send_sem=kv_send.at[which, step - 1],
                    recv_sem=kv_recv.at[which, step - 1],
                    device_id={"ctx": ctx_at(step)},
                    device_id_type=MESH,
                )
            )
        return found

    for step in range(1, REACH + 1):
        for copy in kv_copies(step):
            copy.start()

    def part_copy(step):
        return pltpu.make_async_remote_copy(
            src_ref=part_out.at[step - 1],
            dst_ref=part_in.at[step - 1],
            send_sem=part_send.at[step - 1],
            recv_sem=part_recv.at[step - 1],
            device_id={"ctx": ctx_at(-step)},
            device_id_type=MESH,
        )

    def scatter_copy(which, src, dst, first, high, offset):
        to = tp_at(offset)
        return pltpu.make_async_remote_copy(
            src_ref=src.at[pl.ds(first, high), pl.ds(pl.multiple_of(to * chunk, chunk), chunk)],
            dst_ref=dst.at[offset, pl.ds(first, high)],
            send_sem=tp_send.at[which, offset],
            recv_sem=tp_recv.at[which, offset],
            device_id={"tp": to},
            device_id_type=MESH,
        )

    mine = pl.ds(pl.multiple_of(t * chunk, chunk), chunk)

    def gather_copy(which, ref, first, high, offset):
        place = ref.at[pl.ds(first, high), mine]
        return pltpu.make_async_remote_copy(
            src_ref=place,
            dst_ref=place,
            send_sem=tp_send.at[which, offset],
            recv_sem=tp_recv.at[which, offset],
            device_id={"tp": tp_at(offset)},
            device_id_type=MESH,
        )

    def scatter_start(which, src, dst, first, high):
        for offset in range(1, n_tp):
            scatter_copy(which, src, dst, first, high, offset).start()

    def scatter_finish(which, src, dst, ref, first, high):
        for offset in range(1, n_tp):
            scatter_copy(which, src, dst, first, high, offset).wait()
        part = src[first : first + high, mine].astype(F32)
        for offset in range(1, n_tp):
            part = part + dst[offset, first : first + high, :].astype(F32)
        ref[first : first + high, mine] = part.astype(BF16)
        for offset in range(1, n_tp):
            gather_copy(which + 1, ref, first, high, offset).start()

    def gather_finish(which, ref, first, high):
        for offset in range(1, n_tp):
            gather_copy(which + 1, ref, first, high, offset).wait()

    low_s[0:HEAD, :] = contract(aq_ref[...], x_ref[...], 0, 1).astype(BF16)
    low_s[HEAD : 2 * HEAD, :] = contract(av_ref[...], x_ref[...], 0, 1).astype(BF16)
    scatter_start(0, low_s, low_r, 0, 2 * HEAD)

    ones = jnp.ones((8, HEAD), BF16)
    for h in range(HEADS_LOCAL):
        cols = slice(h * HEAD, (h + 1) * HEAD)
        span = slice(h * rows, (h + 1) * rows)
        q_st[span, :] = q_ref[:, cols]
        grad = do_ref[:, cols]
        do_st[span, :] = grad
        prod = grad.astype(F32) * o_ref[:, cols].astype(F32)
        high = prod.astype(BF16)
        rest = (prod - high.astype(F32)).astype(BF16)
        delta = contract(ones, high, 1, 1) + contract(ones, rest, 1, 1)
        delta_st[:, span] = delta[0:1, :]
        lse_st[:, span] = lse_ref[h : h + 1, :] * LOG2E

    def first_allowed(block, present):
        ids = seg_ref[...]
        found = jnp.zeros((1, rows), jnp.int32)
        for doc in range(1, 4):
            below = jnp.sum((block < doc).astype(F32), axis=1, keepdims=True)
            found = jnp.where(ids == doc, below.astype(jnp.int32), found)
        return jnp.where(present, found, rows)

    def set_thr(found):
        for h in range(HEADS_LOCAL):
            thr_st[:, h * rows : (h + 1) * rows] = found

    def tile(keys, values, sum_k, sum_v, k0, kt, r0, rt, causal):
        ks, rs = slice(k0, k0 + kt), slice(r0, r0 + rt)
        key, value = keys[ks, :], values[ks, :]
        query, grad = q_st[rs, :], do_st[rs, :]
        j = lax.broadcasted_iota(jnp.int32, (kt, rt), 0) + k0
        mask = j >= thr_st[:, rs]
        if causal:
            i = lax.broadcasted_iota(jnp.int32, (1, rt), 1) + (r0 % rows)
            mask = mask & (j <= i)
        score = contract(key, query, 1, 1)
        dprob = contract(value, grad, 1, 1)
        prob = jnp.where(mask, jnp.exp2(score * (SCORE_SCALE * LOG2E) - lse_st[:, rs]), 0.0)
        dscore = (prob * (dprob - delta_st[:, rs])).astype(BF16)
        sum_v[ks, :] += contract(prob.astype(BF16), grad, 1, 0)
        sum_k[ks, :] += contract(dscore, query, 1, 0)
        dq_acc[:, rs] += contract(key, dscore, 0, 0)

    edge = min(256, rows)
    wide = min(512, rows)

    dq_acc[...] = jnp.zeros_like(dq_acc)
    dk_own[...] = jnp.zeros_like(dk_own)
    dv_own[...] = jnp.zeros_like(dv_own)
    set_thr(first_allowed(seg_ref[...], True))
    for h in range(HEADS_LOCAL):
        for r in range(0, rows, edge):
            if r:
                tile(k_ref, v_ref, dk_own, dv_own, 0, r, h * rows + r, edge, False)
            tile(k_ref, v_ref, dk_own, dv_own, r, edge, h * rows + r, edge, True)

    scatter_finish(0, low_s, low_r, low_g, 0, 2 * HEAD)

    def open_step(step):
        for copy in kv_copies(step):
            copy.wait()
        dk_acc[...] = jnp.zeros_like(dk_acc)
        dv_acc[...] = jnp.zeros_like(dv_acc)
        return first_allowed(seg_in[step - 1], c >= step)

    def close_step(step):
        part_out[step - 1, 0] = (SCORE_SCALE * dk_acc[...]).astype(BF16)
        part_out[step - 1, 1] = dv_acc[...].astype(BF16)
        part_copy(step).start()

    def full_step(step, carry):
        set_thr(open_step(step))
        keys, values = k_in.at[step - 1], v_in.at[step - 1]
        for r in range(0, HEADS_LOCAL * rows, wide):
            for k0 in range(0, rows, wide):
                tile(keys, values, dk_acc, dv_acc, k0, wide, r, wide, False)
        close_step(step)
        return carry

    lax.fori_loop(1, REACH, full_step, 0)

    i = lax.broadcasted_iota(jnp.int32, (1, rows), 1)
    set_thr(jnp.maximum(open_step(REACH), i + 1))
    for h in range(HEADS_LOCAL):
        for r in range(0, rows, edge):
            tile(
                k_in.at[REACH - 1], v_in.at[REACH - 1], dk_acc, dv_acc,
                r, rows - r, h * rows + r, edge, False,
            )
    close_step(REACH)

    token_scale = 1.0 / math.sqrt(rows * n_ctx)

    dq_low[...] = (SCORE_SCALE * dq_acc[...]).astype(BF16)
    back_s[0:HEAD, :] = (
        contract(bq_ref[:, 0:HEAD], dq_low[:, 0:rows], 1, 0)
        + contract(bq_ref[:, HEAD : 2 * HEAD], dq_low[:, rows : 2 * rows], 1, 0)
    ).astype(BF16)
    scatter_start(2, back_s, back_r, 0, HEAD)
    gather_finish(0, low_g, 0, 2 * HEAD)
    base = 2 * width
    for h in range(HEADS_LOCAL):
        g_all[base + h * HEAD : base + (h + 1) * HEAD, :] = token_scale * contract(
            dq_low[:, h * rows : (h + 1) * rows], low_g[0:HEAD, :], 1, 1
        )
    scatter_finish(2, back_s, back_r, back_g, 0, HEAD)

    dk_sum = SCORE_SCALE * dk_own[...]
    dv_sum = dv_own[...]
    for step in range(1, REACH + 1):
        part_copy(step).wait()
        dv_sum = dv_sum + part_in[step - 1, 1].astype(F32)
    dv_low[...] = dv_sum.astype(BF16)
    back_s[HEAD : 2 * HEAD, :] = contract(bv_ref[...], dv_low[...], 1, 1).astype(BF16)
    scatter_start(4, back_s, back_r, HEAD, HEAD)
    for step in range(1, REACH + 1):
        dk_sum = dk_sum + part_in[step - 1, 0].astype(F32)
    key_grad_ref[...] = dk_sum.astype(BF16)
    g_all[total - HEAD : total, :] = token_scale * contract(
        low_g[HEAD : 2 * HEAD, :], dv_low[...], 1, 0
    )
    gather_finish(2, back_g, 0, HEAD)
    g_all[0:width, :] = token_scale * contract(back_g[0:HEAD, :], x_ref[...], 1, 0).T
    scatter_finish(4, back_s, back_r, back_g, HEAD, HEAD)
    gather_finish(4, back_g, HEAD, HEAD)
    g_all[width : 2 * width, :] = (
        token_scale * contract(back_g[HEAD : 2 * HEAD, :], x_ref[...], 1, 0).T
    )

    other = 1 - core
    own_half = pl.ds(pl.multiple_of(core * half, 16), half)
    half_s[...] = g_all[pl.ds(pl.multiple_of(other * half, 16), half), :].astype(BF16)

    def to_other(which, src, dst):
        return pltpu.make_async_remote_copy(
            src_ref=src,
            dst_ref=dst,
            send_sem=half_send.at[which],
            recv_sem=half_recv.at[which],
            device_id={"ctx": c + other - core},
            device_id_type=MESH,
        )

    swap = to_other(0, half_s, half_r)
    swap.start()
    swap.wait()
    g_all[0:half, :] = g_all[own_half, :] + half_r[...].astype(F32)
    piece_s[...] = g_all[0:half, :].astype(BF16)

    def piece_copy(offset):
        to = lax.rem(pair + offset, pairs)
        return pltpu.make_async_remote_copy(
            src_ref=piece_s.at[pl.ds(pl.multiple_of(to * piece, 16), piece)],
            dst_ref=piece_r.at[offset],
            send_sem=piece_send.at[0, offset],
            recv_sem=piece_recv.at[0, offset],
            device_id={"ctx": 2 * to + core},
            device_id_type=MESH,
        )

    for offset in range(1, pairs):
        piece_copy(offset).start()
    summed = g_all[pl.ds(pl.multiple_of(pair * piece, 16), piece), :]
    for offset in range(1, pairs):
        piece_copy(offset).wait()
        summed = summed + piece_r[offset].astype(F32)
    own_piece = pl.ds(pl.multiple_of(core * half + pair * piece, 16), piece)
    g_out[own_piece, :] = summed.astype(BF16)

    def spread_copy(offset):
        to = lax.rem(pair + offset, pairs)
        return pltpu.make_async_remote_copy(
            src_ref=g_out.at[own_piece],
            dst_ref=g_out.at[own_piece],
            send_sem=piece_send.at[1, offset],
            recv_sem=piece_recv.at[1, offset],
            device_id={"ctx": 2 * to + core},
            device_id_type=MESH,
        )

    for offset in range(1, pairs):
        spread_copy(offset).start()
    for offset in range(1, pairs):
        spread_copy(offset).wait()
    swap = to_other(1, g_out.at[own_half], g_out.at[own_half])
    swap.start()
    swap.wait()

    ga_q_ref[...] = g_out[0:width, :].astype(F32)
    ga_v_ref[...] = g_out[width : 2 * width, :].astype(F32)
    for h in range(HEADS_LOCAL):
        gb_q_ref[:, h * HEAD : (h + 1) * HEAD] = (
            g_out[base + h * HEAD : base + (h + 1) * HEAD, :].astype(F32).T
        )
    gb_v_ref[...] = g_out[total - HEAD : total, :].astype(F32)


def per_device(x, q, k, v, do, o, lse, seg, aq, bq, av, bv):
    n_ctx, n_tp = lax.axis_size("ctx"), lax.axis_size("tp")
    rows, width = x.shape
    chunk = rows // n_tp
    total = 2 * width + 3 * HEAD
    half = total // 2
    pairs = n_ctx // 2
    piece = half // pairs
    dma = pltpu.SemaphoreType.DMA
    vmem = pltpu.VMEM
    scratch = [
        vmem((REACH, rows, HEAD), BF16),
        vmem((REACH, rows, HEAD), BF16),
        vmem((REACH, 1, rows), jnp.int32),
        vmem((2 * rows, HEAD), BF16),
        vmem((2 * rows, HEAD), BF16),
        vmem((1, 2 * rows), F32),
        vmem((1, 2 * rows), F32),
        vmem((1, 2 * rows), jnp.int32),
        vmem((rows, HEAD), F32),
        vmem((rows, HEAD), F32),
        vmem((rows, HEAD), F32),
        vmem((rows, HEAD), F32),
        vmem((HEAD, 2 * rows), F32),
        vmem((HEAD, 2 * rows), BF16),
        vmem((rows, HEAD), BF16),
        vmem((REACH, 2, rows, HEAD), BF16),
        vmem((REACH, 2, rows, HEAD), BF16),
        vmem((2 * HEAD, rows), BF16),
        vmem((n_tp, 2 * HEAD, chunk), BF16),
        vmem((2 * HEAD, rows), BF16),
        vmem((2 * HEAD, rows), BF16),
        vmem((n_tp, 2 * HEAD, chunk), BF16),
        vmem((2 * HEAD, rows), BF16),
        vmem((total, HEAD), F32),
        vmem((half, HEAD), BF16),
        vmem((half, HEAD), BF16),
        vmem((half, HEAD), BF16),
        vmem((pairs, piece, HEAD), BF16),
        vmem((total, HEAD), BF16),
        dma((3, REACH)),
        dma((3, REACH)),
        dma((REACH,)),
        dma((REACH,)),
        dma((6, n_tp)),
        dma((6, n_tp)),
        dma((2,)),
        dma((2,)),
        dma((2, pairs)),
        dma((2, pairs)),
    ]
    whole = pl.BlockSpec(memory_space=pltpu.VMEM)
    flops = 10 * 9 * rows * rows * HEAD
    return pl.pallas_call(
        functools.partial(kernel, n_ctx, n_tp),
        out_shape=[
            jax.ShapeDtypeStruct((rows, HEAD), BF16),
            jax.ShapeDtypeStruct((width, HEAD), F32),
            jax.ShapeDtypeStruct((HEAD, 2 * HEAD), F32),
            jax.ShapeDtypeStruct((width, HEAD), F32),
            jax.ShapeDtypeStruct((HEAD, HEAD), F32),
        ],
        in_specs=[whole] * 12,
        out_specs=[whole] * 5,
        scratch_shapes=scratch,
        compiler_params=pltpu.CompilerParams(
            collective_id=0, has_side_effects=True, vmem_limit_bytes=56 * 1024 * 1024
        ),
        cost_estimate=pl.CostEstimate(
            flops=flops, bytes_accessed=8 * 1024 * 1024, transcendentals=9 * rows * rows
        ),
    )(x, q, k, v, do, o, lse, seg.reshape(1, rows), aq, bq, av, bv)


def solution(mesh):
    placed = (
        P("ctx", "tp"),
        P("ctx", "tp"),
        P("ctx", "tp"),
        P("ctx", "tp"),
        P("ctx", "tp"),
        P("ctx", "tp"),
        P("tp", "ctx"),
        P("ctx"),
        P("tp", None),
        P(None, "tp"),
        P("tp", None),
        P(None, "tp"),
    )
    return jax.shard_map(
        per_device,
        mesh=mesh,
        in_specs=placed,
        out_specs=(P("ctx", "tp"), P("tp", None), P(None, "tp"), P("tp", None), P(None, "tp")),
        check_vma=False,
    )
```

```python
import functools
import math

import jax
import jax.numpy as jnp
from jax import lax
from jax.experimental import pallas as pl
from jax.experimental.pallas import tpu as pltpu
from jax.sharding import PartitionSpec as P

HEAD = 128
HEADS_LOCAL = 2
REACH = 4
SCORE_SCALE = 144.0 ** (-0.5)
LOG2E = 1.4426950408889634
BF16 = jnp.bfloat16
F32 = jnp.float32
MESH = pl.DeviceIdType.MESH


def contract(a, b, dim_a, dim_b):
    return lax.dot_general(
        a, b, (((dim_a,), (dim_b,)), ((), ())), preferred_element_type=F32
    )


def kernel(
    n_ctx,
    n_tp,
    x_hbm,
    q_hbm,
    k_hbm,
    v_hbm,
    do_hbm,
    o_hbm,
    lse_hbm,
    seg_hbm,
    aq_hbm,
    bq_hbm,
    av_hbm,
    bv_hbm,
    key_grad_ref,
    sums_ref,
    x_ref,
    q_ref,
    k_ref,
    v_ref,
    do_ref,
    o_ref,
    lse_ref,
    seg_ref,
    aq_ref,
    bq_ref,
    av_ref,
    bv_ref,
    load_sem,
    k_in,
    v_in,
    seg_in,
    q_st,
    do_st,
    lse_st,
    delta_st,
    thr_st,
    acc,
    own,
    dq_acc,
    dq_low,
    dv_low,
    part_out,
    part_in,
    low_s,
    low_r,
    low_g,
    back_s,
    back_r,
    back_g,
    g_all,
    half_s,
    half_r,
    piece_s,
    piece_r,
    g_out,
    kv_send,
    kv_recv,
    part_send,
    part_recv,
    tp_send,
    tp_recv,
    half_send,
    half_recv,
    piece_send,
    piece_recv,
):
    rows = k_ref.shape[0]
    width = x_ref.shape[0]
    chunk = rows // n_tp
    pairs = n_ctx // 2
    total = g_all.shape[0]
    half = total // 2
    piece = half // pairs
    c = lax.axis_index("ctx")
    t = lax.axis_index("tp")
    core = lax.rem(c, 2)
    pair = c // 2
    side = lax.rem(pair, 2)

    def ctx_at(offset):
        return lax.rem(c + (offset + n_ctx), n_ctx)

    def tp_at(offset):
        return lax.rem(t + offset, n_tp)

    barrier = pltpu.get_barrier_semaphore()
    offsets = {s % n_ctx for s in range(-REACH, REACH + 1)} | set(range(0, n_ctx, 2))
    offsets = sorted(offsets - {0})
    for offset in offsets:
        pl.semaphore_signal(
            barrier, inc=1, device_id={"ctx": ctx_at(offset)}, device_id_type=MESH
        )
    for offset in range(1, n_tp):
        pl.semaphore_signal(
            barrier, inc=1, device_id={"tp": tp_at(offset)}, device_id_type=MESH
        )
    loads = {}
    for place, (src, dst) in enumerate(
        (
            (k_hbm, k_ref),
            (v_hbm, v_ref),
            (seg_hbm, seg_ref),
            (aq_hbm, aq_ref),
            (av_hbm, av_ref),
            (x_hbm, x_ref),
            (q_hbm, q_ref),
            (do_hbm, do_ref),
            (o_hbm, o_ref),
            (lse_hbm, lse_ref),
            (bq_hbm, bq_ref),
            (bv_hbm, bv_ref),
        )
    ):
        loads[place] = pltpu.make_async_copy(src, dst, load_sem.at[place])
        loads[place].start()
    for place in range(6):
        loads[place].wait()
    low_s[0:HEAD, :] = contract(aq_ref[...], x_ref[...], 0, 0).astype(BF16)
    low_s[HEAD : 2 * HEAD, :] = contract(av_ref[...], x_ref[...], 0, 0).astype(BF16)
    pl.semaphore_wait(barrier, len(offsets) + n_tp - 1)

    cross_core = c + 1 - 2 * core
    cross_x = c + 2 - 4 * side
    sources = (seg_ref, k_ref, v_ref)
    landed = (seg_in, k_in, v_in)

    def kv_copy(which, slot, target, relay=None):
        src = sources[which] if relay is None else landed[which].at[relay]
        return pltpu.make_async_remote_copy(
            src_ref=src,
            dst_ref=landed[which].at[slot],
            send_sem=kv_send.at[which, slot],
            recv_sem=kv_recv.at[which, slot],
            device_id={"ctx": target},
            device_id_type=MESH,
        )

    for which in range(3):
        kv_copy(which, 0, ctx_at(REACH)).start()

        @pl.when(core == 0)
        def _(which=which):
            kv_copy(which, 1, cross_core).start()

        @pl.when(side == 0)
        def _(which=which):
            kv_copy(which, 2, cross_x).start()

    def part_copy(slot, which, target):
        return pltpu.make_async_remote_copy(
            src_ref=part_out.at[slot, which],
            dst_ref=part_in.at[slot, which],
            send_sem=part_send.at[slot, which],
            recv_sem=part_recv.at[slot, which],
            device_id={"ctx": target},
            device_id_type=MESH,
        )

    def scatter_copy(which, src, dst, first, high, offset):
        to = tp_at(offset)
        return pltpu.make_async_remote_copy(
            src_ref=src.at[pl.ds(first, high), pl.ds(pl.multiple_of(to * chunk, chunk), chunk)],
            dst_ref=dst.at[offset, pl.ds(first, high)],
            send_sem=tp_send.at[which, offset],
            recv_sem=tp_recv.at[which, offset],
            device_id={"tp": to},
            device_id_type=MESH,
        )

    mine = pl.ds(pl.multiple_of(t * chunk, chunk), chunk)

    def gather_copy(which, ref, first, high, offset):
        place = ref.at[pl.ds(first, high), mine]
        return pltpu.make_async_remote_copy(
            src_ref=place,
            dst_ref=place,
            send_sem=tp_send.at[which, offset],
            recv_sem=tp_recv.at[which, offset],
            device_id={"tp": tp_at(offset)},
            device_id_type=MESH,
        )

    def scatter_start(which, src, dst, first, high):
        for offset in range(1, n_tp):
            scatter_copy(which, src, dst, first, high, offset).start()

    def scatter_finish(which, src, dst, ref, first, high):
        for offset in range(1, n_tp):
            scatter_copy(which, src, dst, first, high, offset).wait()
        part = src[first : first + high, mine].astype(F32)
        for offset in range(1, n_tp):
            part = part + dst[offset, first : first + high, :].astype(F32)
        ref[first : first + high, mine] = part.astype(BF16)
        for offset in range(1, n_tp):
            gather_copy(which + 1, ref, first, high, offset).start()

    def gather_finish(which, ref, first, high):
        for offset in range(1, n_tp):
            gather_copy(which + 1, ref, first, high, offset).wait()

    scatter_start(0, low_s, low_r, 0, 2 * HEAD)
    for place in range(6, 12):
        loads[place].wait()

    ones = jnp.ones((8, HEAD), BF16)
    for h in range(HEADS_LOCAL):
        cols = slice(h * HEAD, (h + 1) * HEAD)
        span = slice(h * rows, (h + 1) * rows)
        q_st[span, :] = q_ref[:, cols]
        grad = do_ref[:, cols]
        do_st[span, :] = grad
        prod = grad.astype(F32) * o_ref[:, cols].astype(F32)
        high = prod.astype(BF16)
        rest = (prod - high.astype(F32)).astype(BF16)
        delta = contract(ones, high, 1, 1) + contract(ones, rest, 1, 1)
        delta_st[:, span] = delta[0:1, :]
        lse_st[:, span] = lse_ref[h : h + 1, :] * LOG2E

    def first_allowed(block, present):
        ids = seg_ref[...]
        found = jnp.zeros((1, rows), jnp.int32)
        for doc in range(1, 4):
            below = jnp.sum((block < doc).astype(F32), axis=1, keepdims=True)
            found = jnp.where(ids == doc, below.astype(jnp.int32), found)
        return jnp.where(present, found, rows)

    def set_thr(found):
        for h in range(HEADS_LOCAL):
            thr_st[:, h * rows : (h + 1) * rows] = found

    def tile(keys, values, sums, k0, kt, r0, rt, causal):
        ks, rs = slice(k0, k0 + kt), slice(r0, r0 + rt)
        key, value = keys[ks, :], values[ks, :]
        query, grad = q_st[rs, :], do_st[rs, :]
        j = lax.broadcasted_iota(jnp.int32, (kt, rt), 0) + k0
        mask = j >= thr_st[:, rs]
        if causal:
            i = lax.broadcasted_iota(jnp.int32, (1, rt), 1) + (r0 % rows)
            mask = mask & (j <= i)
        score = contract(key, query, 1, 1)
        dprob = contract(value, grad, 1, 1)
        prob = jnp.where(mask, jnp.exp2(score * (SCORE_SCALE * LOG2E) - lse_st[:, rs]), 0.0)
        dscore = (prob * (dprob - delta_st[:, rs])).astype(BF16)
        sums[0, ks, :] += contract(prob.astype(BF16), grad, 1, 0)
        sums[1, ks, :] += contract(dscore, query, 1, 0)
        dq_acc[:, rs] += contract(key, dscore, 0, 0)

    edge = min(256, rows)
    wide = min(512, rows)

    dq_acc[...] = jnp.zeros_like(dq_acc)
    own[...] = jnp.zeros_like(own)
    acc[0] = jnp.zeros_like(own)
    set_thr(first_allowed(seg_ref[...], True))
    for h in range(HEADS_LOCAL):
        for r in range(0, rows, edge):
            if r:
                tile(k_ref, v_ref, own, 0, r, h * rows + r, edge, False)
            tile(k_ref, v_ref, own, r, edge, h * rows + r, edge, True)

    scatter_finish(0, low_s, low_r, low_g, 0, 2 * HEAD)

    for which in range(3):
        kv_copy(which, 0, cross_core).wait_recv()

        @pl.when(core == 1)
        def _(which=which):
            kv_copy(which, 1, cross_core, 0).start()

        @pl.when(side == 1)
        def _(which=which):
            kv_copy(which, 2, cross_x, 0).start()

    i = lax.broadcasted_iota(jnp.int32, (1, rows), 1)
    set_thr(jnp.maximum(first_allowed(seg_in[0], c >= REACH), i + 1))
    for h in range(HEADS_LOCAL):
        for r in range(0, rows, edge):
            tile(
                k_in.at[0], v_in.at[0], acc.at[0], r, rows - r, h * rows + r, edge, False
            )

    def full_step(slot, carry):
        for which in range(3):
            kv_copy(which, slot, cross_core).wait_recv()

        @pl.when(slot == 2)
        def _():
            for which in range(3):
                kv_copy(which, 3, cross_core, 2).start()

        back = jnp.where(slot == 2, 2, jnp.where((slot == 1) == (core == 1), 1, 3))
        set_thr(first_allowed(seg_in[slot], c >= back))
        sums = acc.at[2 - lax.rem(slot, 2)]
        sums[...] = jnp.zeros_like(own)
        keys, values = k_in.at[slot], v_in.at[slot]
        for r in range(0, HEADS_LOCAL * rows, wide):
            for k0 in range(0, rows, wide):
                tile(keys, values, sums, k0, wide, r, wide, False)

        @pl.when(slot != 2)
        def _():
            part_out[slot, 0] = acc[1, 0].astype(BF16)
            part_copy(slot, 0, cross_core).start()
            part_out[slot, 1] = (SCORE_SCALE * acc[1, 1]).astype(BF16)
            part_copy(slot, 1, cross_core).start()

        @pl.when(slot == 2)
        def _():
            for which in range(2):
                part_copy(1, which, cross_core).wait()
            second = core == 1
            acc[0, 0] = acc[0, 0] + jnp.where(second, part_in[1, 0].astype(F32), 0.0)
            acc[0, 1] = SCORE_SCALE * acc[0, 1] + jnp.where(
                second, part_in[1, 1].astype(F32), 0.0
            )

            for which in range(2):
                part_out[0, which] = acc[0, which].astype(BF16)
                part_copy(0, which, ctx_at(-REACH)).start()

        return carry

    lax.fori_loop(1, REACH, full_step, 0)

    token_scale = 1.0 / math.sqrt(rows * n_ctx)

    dq_low[...] = (SCORE_SCALE * dq_acc[...]).astype(BF16)
    back_s[0:HEAD, :] = (
        contract(bq_ref[:, 0:HEAD], dq_low[:, 0:rows], 1, 0)
        + contract(bq_ref[:, HEAD : 2 * HEAD], dq_low[:, rows : 2 * rows], 1, 0)
    ).astype(BF16)
    scatter_start(2, back_s, back_r, 0, HEAD)
    part_copy(3, 0, cross_core).wait()
    part_out[2, 0] = (acc[2, 0] + part_in[3, 0].astype(F32)).astype(BF16)
    part_copy(2, 0, ctx_at(-2)).start()

    gather_finish(0, low_g, 0, 2 * HEAD)
    base = 2 * width
    for h in range(HEADS_LOCAL):
        g_all[base + h * HEAD : base + (h + 1) * HEAD, :] = token_scale * contract(
            dq_low[:, h * rows : (h + 1) * rows], low_g[0:HEAD, :], 1, 1
        )
    scatter_finish(2, back_s, back_r, back_g, 0, HEAD)

    def gathered(which):
        near = jnp.where(core == 0, part_in[1, which].astype(F32), 0.0)
        part_copy(0, which, ctx_at(-REACH)).wait()
        part_copy(2, which, ctx_at(-2)).wait()
        return near + part_in[0, which].astype(F32) + part_in[2, which].astype(F32)

    dv_low[...] = (own[0] + gathered(0)).astype(BF16)
    back_s[HEAD : 2 * HEAD, :] = contract(bv_ref[...], dv_low[...], 1, 1).astype(BF16)
    scatter_start(4, back_s, back_r, HEAD, HEAD)
    part_copy(3, 1, cross_core).wait()
    part_out[2, 1] = (SCORE_SCALE * acc[2, 1] + part_in[3, 1].astype(F32)).astype(BF16)
    part_copy(2, 1, ctx_at(-2)).start()
    g_all[total - HEAD : total, :] = token_scale * contract(
        low_g[HEAD : 2 * HEAD, :], dv_low[...], 1, 0
    )
    gather_finish(2, back_g, 0, HEAD)
    g_all[0:width, :] = token_scale * contract(x_ref[...], back_g[0:HEAD, :], 1, 1)

    scatter_finish(4, back_s, back_r, back_g, HEAD, HEAD)
    gather_finish(4, back_g, HEAD, HEAD)
    g_all[width : 2 * width, :] = token_scale * contract(
        x_ref[...], back_g[HEAD : 2 * HEAD, :], 1, 1
    )

    other = 1 - core
    own_half = pl.ds(pl.multiple_of(core * half, 16), half)
    half_s[...] = g_all[pl.ds(pl.multiple_of(other * half, 16), half), :].astype(BF16)

    def to_other(which, src, dst):
        return pltpu.make_async_remote_copy(
            src_ref=src,
            dst_ref=dst,
            send_sem=half_send.at[which],
            recv_sem=half_recv.at[which],
            device_id={"ctx": c + other - core},
            device_id_type=MESH,
        )

    swap = to_other(0, half_s, half_r)
    swap.start()
    swap.wait()
    g_all[0:half, :] = g_all[own_half, :] + half_r[...].astype(F32)
    piece_s[...] = g_all[0:half, :].astype(BF16)

    def piece_copy(offset):
        to = lax.rem(pair + offset, pairs)
        return pltpu.make_async_remote_copy(
            src_ref=piece_s.at[pl.ds(pl.multiple_of(to * piece, 16), piece)],
            dst_ref=piece_r.at[offset],
            send_sem=piece_send.at[0, offset],
            recv_sem=piece_recv.at[0, offset],
            device_id={"ctx": 2 * to + core},
            device_id_type=MESH,
        )

    for offset in range(1, pairs):
        piece_copy(offset).start()
    summed = g_all[pl.ds(pl.multiple_of(pair * piece, 16), piece), :]
    for offset in range(1, pairs):
        piece_copy(offset).wait()
        summed = summed + piece_r[offset].astype(F32)
    own_piece = pl.ds(pl.multiple_of(core * half + pair * piece, 16), piece)
    g_out[own_piece, :] = summed.astype(BF16)

    def spread_copy(offset):
        to = lax.rem(pair + offset, pairs)
        return pltpu.make_async_remote_copy(
            src_ref=g_out.at[own_piece],
            dst_ref=g_out.at[own_piece],
            send_sem=piece_send.at[1, offset],
            recv_sem=piece_recv.at[1, offset],
            device_id={"ctx": 2 * to + core},
            device_id_type=MESH,
        )

    for offset in range(1, pairs):
        spread_copy(offset).start()
    for offset in range(1, pairs):
        spread_copy(offset).wait()
    swap = to_other(1, g_out.at[own_half], g_out.at[own_half])
    swap.start()
    swap.wait()

    sums_ref[...] = g_out[...]
    key_grad_ref[...] = (SCORE_SCALE * own[1] + gathered(1)).astype(BF16)
    for which in range(3):
        for slot in range(REACH):
            kv_copy(which, slot, cross_core).wait_send()


def finish(key_ref, sums_ref, key_grad_ref, ga_q_ref, gb_q_ref, ga_v_ref, gb_v_ref):
    key_grad_ref[...] = key_ref[...]
    width = ga_q_ref.shape[0]
    base = 2 * width
    ga_q_ref[...] = sums_ref[0:width, :].astype(F32)
    ga_v_ref[...] = sums_ref[width : 2 * width, :].astype(F32)
    for h in range(HEADS_LOCAL):
        gb_q_ref[:, h * HEAD : (h + 1) * HEAD] = (
            sums_ref[base + h * HEAD : base + (h + 1) * HEAD, :].astype(F32).T
        )
    gb_v_ref[...] = sums_ref[base + HEADS_LOCAL * HEAD :, :].astype(F32)


def per_device(x, q, k, v, do, o, lse, seg, aq, bq, av, bv):
    n_ctx, n_tp = lax.axis_size("ctx"), lax.axis_size("tp")
    rows, width = x.shape
    chunk = rows // n_tp
    total = 2 * width + 3 * HEAD
    half = total // 2
    pairs = n_ctx // 2
    piece = half // pairs
    dma = pltpu.SemaphoreType.DMA
    vmem = pltpu.VMEM
    scratch = [
        vmem((width, rows), BF16),
        vmem((rows, 2 * HEAD), BF16),
        vmem((rows, HEAD), BF16),
        vmem((rows, HEAD), BF16),
        vmem((rows, 2 * HEAD), BF16),
        vmem((rows, 2 * HEAD), BF16),
        vmem((2, rows), F32),
        vmem((1, rows), jnp.int32),
        vmem((width, HEAD), BF16),
        vmem((HEAD, 2 * HEAD), BF16),
        vmem((width, HEAD), BF16),
        vmem((HEAD, HEAD), BF16),
        dma((12,)),
        vmem((REACH, rows, HEAD), BF16),
        vmem((REACH, rows, HEAD), BF16),
        vmem((REACH, 1, rows), jnp.int32),
        vmem((2 * rows, HEAD), BF16),
        vmem((2 * rows, HEAD), BF16),
        vmem((1, 2 * rows), F32),
        vmem((1, 2 * rows), F32),
        vmem((1, 2 * rows), jnp.int32),
        vmem((3, 2, rows, HEAD), F32),
        vmem((2, rows, HEAD), F32),
        vmem((HEAD, 2 * rows), F32),
        vmem((HEAD, 2 * rows), BF16),
        vmem((rows, HEAD), BF16),
        vmem((REACH, 2, rows, HEAD), BF16),
        vmem((REACH, 2, rows, HEAD), BF16),
        vmem((2 * HEAD, rows), BF16),
        vmem((n_tp, 2 * HEAD, chunk), BF16),
        vmem((2 * HEAD, rows), BF16),
        vmem((2 * HEAD, rows), BF16),
        vmem((n_tp, 2 * HEAD, chunk), BF16),
        vmem((2 * HEAD, rows), BF16),
        vmem((total, HEAD), F32),
        vmem((half, HEAD), BF16),
        vmem((half, HEAD), BF16),
        vmem((half, HEAD), BF16),
        vmem((pairs, piece, HEAD), BF16),
        vmem((total, HEAD), BF16),
        dma((3, REACH)),
        dma((3, REACH)),
        dma((REACH, 2)),
        dma((REACH, 2)),
        dma((6, n_tp)),
        dma((6, n_tp)),
        dma((2,)),
        dma((2,)),
        dma((2, pairs)),
        dma((2, pairs)),
    ]
    whole = pl.BlockSpec(memory_space=pltpu.VMEM)
    flops = 10 * 9 * rows * rows * HEAD
    key_grad, sums = pl.pallas_call(
        functools.partial(kernel, n_ctx, n_tp),
        out_shape=[
            jax.ShapeDtypeStruct((rows, HEAD), BF16),
            jax.ShapeDtypeStruct((total, HEAD), BF16),
        ],
        in_specs=[pl.BlockSpec(memory_space=pl.ANY)] * 12,
        out_specs=[whole] * 2,
        scratch_shapes=scratch,
        compiler_params=pltpu.CompilerParams(
            collective_id=0, has_side_effects=True, vmem_limit_bytes=56 * 1024 * 1024
        ),
        cost_estimate=pl.CostEstimate(
            flops=flops, bytes_accessed=8 * 1024 * 1024, transcendentals=9 * rows * rows
        ),
    )(x.T, q, k, v, do, o, lse, seg.reshape(1, rows), aq, bq, av, bv)
    return pl.pallas_call(
        finish,
        out_shape=[
            jax.ShapeDtypeStruct((rows, HEAD), BF16),
            jax.ShapeDtypeStruct((width, HEAD), F32),
            jax.ShapeDtypeStruct((HEAD, 2 * HEAD), F32),
            jax.ShapeDtypeStruct((width, HEAD), F32),
            jax.ShapeDtypeStruct((HEAD, HEAD), F32),
        ],
        in_specs=[whole] * 2,
        out_specs=[whole] * 5,
    )(key_grad, sums)


def solution(mesh):
    placed = (
        P("ctx", "tp"),
        P("ctx", "tp"),
        P("ctx", "tp"),
        P("ctx", "tp"),
        P("ctx", "tp"),
        P("ctx", "tp"),
        P("tp", "ctx"),
        P("ctx"),
        P("tp", None),
        P(None, "tp"),
        P("tp", None),
        P(None, "tp"),
    )
    return jax.shard_map(
        per_device,
        mesh=mesh,
        in_specs=placed,
        out_specs=(P("ctx", "tp"), P("tp", None), P(None, "tp"), P("tp", None), P(None, "tp")),
        check_vma=False,
    )
```

```python
import functools
import math

import jax
import jax.numpy as jnp
from jax import lax
from jax.experimental import pallas as pl
from jax.experimental.pallas import tpu as pltpu
from jax.sharding import PartitionSpec as P

HEAD = 128
HEADS_LOCAL = 2
REACH = 4
SCORE_SCALE = 144.0 ** (-0.5)
LOG2E = 1.4426950408889634
BF16 = jnp.bfloat16
F32 = jnp.float32
MESH = pl.DeviceIdType.MESH


def contract(a, b, dim_a, dim_b):
    return lax.dot_general(
        a, b, (((dim_a,), (dim_b,)), ((), ())), preferred_element_type=F32
    )


def kernel(
    n_ctx,
    n_tp,
    x_hbm,
    q_hbm,
    k_hbm,
    v_hbm,
    do_hbm,
    o_hbm,
    lse_hbm,
    seg_hbm,
    aq_hbm,
    bq_hbm,
    av_hbm,
    bv_hbm,
    key_grad_ref,
    sums_ref,
    x_ref,
    q_ref,
    k_ref,
    v_ref,
    do_ref,
    o_ref,
    lse_ref,
    seg_ref,
    aq_ref,
    bq_ref,
    av_ref,
    bv_ref,
    load_sem,
    k_in,
    v_in,
    seg_in,
    q_st,
    do_st,
    lse_st,
    delta_st,
    thr_st,
    acc,
    own,
    dq_acc,
    dq_low,
    dv_low,
    part_out,
    part_in,
    low_s,
    low_r,
    low_g,
    back_s,
    back_r,
    back_g,
    g_all,
    half_s,
    half_r,
    piece_s,
    piece_r,
    g_out,
    kv_send,
    kv_recv,
    part_send,
    part_recv,
    tp_send,
    tp_recv,
    half_send,
    half_recv,
    piece_send,
    piece_recv,
):
    rows = k_ref.shape[0]
    width = x_ref.shape[0]
    chunk = rows // n_tp
    pairs = n_ctx // 2
    total = g_all.shape[0]
    half = total // 2
    piece = half // pairs
    c = lax.axis_index("ctx")
    t = lax.axis_index("tp")
    core = lax.rem(c, 2)
    pair = c // 2
    side = lax.rem(pair, 2)

    def ctx_at(offset):
        return lax.rem(c + (offset + n_ctx), n_ctx)

    def tp_at(offset):
        return lax.rem(t + offset, n_tp)

    barrier = pltpu.get_barrier_semaphore()
    offsets = {s % n_ctx for s in range(-REACH, REACH + 1)} | set(range(0, n_ctx, 2))
    offsets = sorted(offsets - {0})
    for offset in offsets:
        pl.semaphore_signal(
            barrier, inc=1, device_id={"ctx": ctx_at(offset)}, device_id_type=MESH
        )
    for offset in range(1, n_tp):
        pl.semaphore_signal(
            barrier, inc=1, device_id={"tp": tp_at(offset)}, device_id_type=MESH
        )
    loads = {}
    for place, (src, dst) in enumerate(
        (
            (k_hbm, k_ref),
            (v_hbm, v_ref),
            (seg_hbm, seg_ref),
            (aq_hbm, aq_ref),
            (av_hbm, av_ref),
            (x_hbm, x_ref),
            (q_hbm, q_ref),
            (do_hbm, do_ref),
            (o_hbm, o_ref),
            (lse_hbm, lse_ref),
            (bq_hbm, bq_ref),
            (bv_hbm, bv_ref),
        )
    ):
        loads[place] = pltpu.make_async_copy(src, dst, load_sem.at[place])
        loads[place].start()
    for place in range(6):
        loads[place].wait()
    low_s[0:HEAD, :] = contract(aq_ref[...], x_ref[...], 0, 0).astype(BF16)
    low_s[HEAD : 2 * HEAD, :] = contract(av_ref[...], x_ref[...], 0, 0).astype(BF16)
    pl.semaphore_wait(barrier, len(offsets) + n_tp - 1)

    cross_core = c + 1 - 2 * core
    cross_x = c + 2 - 4 * side
    mid = rows // 2
    pieces = ((seg_ref, seg_in, None), (k_ref, k_in, 0), (v_ref, v_in, 0), (k_ref, k_in, 1), (v_ref, v_in, 1))
    groups = ((0, 1, 2), (3, 4))

    def kv_copy(which, slot, target, relay=None):
        src, dst, part = pieces[which]
        src = src if relay is None else dst.at[relay]
        dst = dst.at[slot]
        if part is not None:
            src, dst = src.at[pl.ds(part * mid, mid)], dst.at[pl.ds(part * mid, mid)]
        return pltpu.make_async_remote_copy(
            src_ref=src,
            dst_ref=dst,
            send_sem=kv_send.at[which, slot],
            recv_sem=kv_recv.at[which, slot],
            device_id={"ctx": target},
            device_id_type=MESH,
        )

    def arrived(slot, part):
        for which in groups[part]:
            kv_copy(which, slot, cross_core).wait_recv()

    for which in range(5):
        kv_copy(which, 0, ctx_at(REACH)).start()

        @pl.when(core == 0)
        def _(which=which):
            kv_copy(which, 1, cross_core).start()

        @pl.when(side == 0)
        def _(which=which):
            kv_copy(which, 2, cross_x).start()

    def hand_on(part):
        for which in groups[part]:
            kv_copy(which, 0, cross_core).wait_recv()

            @pl.when(core == 1)
            def _(which=which):
                kv_copy(which, 1, cross_core, 0).start()

            @pl.when(side == 1)
            def _(which=which):
                kv_copy(which, 2, cross_x, 0).start()

    def part_copy(slot, which, target, part=None):
        src, dst = part_out.at[slot, which], part_in.at[slot, which]
        place = 2 * which
        if part is not None:
            src, dst = src.at[pl.ds(part * mid, mid)], dst.at[pl.ds(part * mid, mid)]
            place = place + part
        return pltpu.make_async_remote_copy(
            src_ref=src,
            dst_ref=dst,
            send_sem=part_send.at[slot, place],
            recv_sem=part_recv.at[slot, place],
            device_id={"ctx": target},
            device_id_type=MESH,
        )

    def scatter_copy(which, src, dst, first, high, offset):
        to = tp_at(offset)
        return pltpu.make_async_remote_copy(
            src_ref=src.at[pl.ds(first, high), pl.ds(pl.multiple_of(to * chunk, chunk), chunk)],
            dst_ref=dst.at[offset, pl.ds(first, high)],
            send_sem=tp_send.at[which, offset],
            recv_sem=tp_recv.at[which, offset],
            device_id={"tp": to},
            device_id_type=MESH,
        )

    mine = pl.ds(pl.multiple_of(t * chunk, chunk), chunk)

    def gather_copy(which, ref, first, high, offset):
        place = ref.at[pl.ds(first, high), mine]
        return pltpu.make_async_remote_copy(
            src_ref=place,
            dst_ref=place,
            send_sem=tp_send.at[which, offset],
            recv_sem=tp_recv.at[which, offset],
            device_id={"tp": tp_at(offset)},
            device_id_type=MESH,
        )

    def scatter_start(which, src, dst, first, high):
        for offset in range(1, n_tp):
            scatter_copy(which, src, dst, first, high, offset).start()

    def scatter_finish(which, src, dst, ref, first, high):
        for offset in range(1, n_tp):
            scatter_copy(which, src, dst, first, high, offset).wait()
        part = src[first : first + high, mine].astype(F32)
        for offset in range(1, n_tp):
            part = part + dst[offset, first : first + high, :].astype(F32)
        ref[first : first + high, mine] = part.astype(BF16)
        for offset in range(1, n_tp):
            gather_copy(which + 1, ref, first, high, offset).start()

    def gather_finish(which, ref, first, high):
        for offset in range(1, n_tp):
            gather_copy(which + 1, ref, first, high, offset).wait()

    for place in range(6, 12):
        loads[place].wait()

    ones = jnp.ones((8, HEAD), BF16)
    for h in range(HEADS_LOCAL):
        cols = slice(h * HEAD, (h + 1) * HEAD)
        span = slice(h * rows, (h + 1) * rows)
        q_st[span, :] = q_ref[:, cols]
        grad = do_ref[:, cols]
        do_st[span, :] = grad
        prod = grad.astype(F32) * o_ref[:, cols].astype(F32)
        high = prod.astype(BF16)
        rest = (prod - high.astype(F32)).astype(BF16)
        delta = contract(ones, high, 1, 1) + contract(ones, rest, 1, 1)
        delta_st[:, span] = delta[0:1, :]
        lse_st[:, span] = lse_ref[h : h + 1, :] * LOG2E

    def first_allowed(block, present):
        ids = seg_ref[...]
        found = jnp.zeros((1, rows), jnp.int32)
        for doc in range(1, 4):
            below = jnp.sum((block < doc).astype(F32), axis=1, keepdims=True)
            found = jnp.where(ids == doc, below.astype(jnp.int32), found)
        return jnp.where(present, found, rows)

    def set_thr(found):
        for h in range(HEADS_LOCAL):
            thr_st[:, h * rows : (h + 1) * rows] = found

    def tile(keys, values, sums, k0, kt, r0, rt, causal):
        ks, rs = pl.ds(k0, kt), pl.ds(r0, rt)
        key, value = keys[ks, :], values[ks, :]
        query, grad = q_st[rs, :], do_st[rs, :]
        j = lax.broadcasted_iota(jnp.int32, (kt, rt), 0) + k0
        mask = j >= thr_st[:, rs]
        if causal:
            i = lax.broadcasted_iota(jnp.int32, (1, rt), 1) + (r0 % rows)
            mask = mask & (j <= i)
        score = contract(key, query, 1, 1)
        dprob = contract(value, grad, 1, 1)
        prob = jnp.where(mask, jnp.exp2(score * (SCORE_SCALE * LOG2E) - lse_st[:, rs]), 0.0)
        dscore = (prob * (dprob - delta_st[:, rs])).astype(BF16)
        sums[0, ks, :] += contract(prob.astype(BF16), grad, 1, 0)
        sums[1, ks, :] += contract(dscore, query, 1, 0)
        dq_acc[:, rs] += contract(key, dscore, 0, 0)

    edge = min(256, rows)
    wide = min(512, rows)

    dq_acc[...] = jnp.zeros_like(dq_acc)
    own[...] = jnp.zeros_like(own)
    acc[0] = jnp.zeros_like(own)
    set_thr(first_allowed(seg_ref[...], True))
    for h in range(HEADS_LOCAL):
        for r in range(0, rows, edge):
            if r:
                tile(k_ref, v_ref, own, 0, r, h * rows + r, edge, False)
            tile(k_ref, v_ref, own, r, edge, h * rows + r, edge, True)

    def half_block(slot, part):
        back = jnp.where(slot == 2, 2, jnp.where((slot == 1) == (core == 1), 1, 3))
        set_thr(first_allowed(seg_in[slot], c >= back))
        k0 = pl.multiple_of(part * mid, mid)
        sums = acc.at[2 - slot % 2]
        for which in range(2):
            sums[which, pl.ds(k0, mid), :] = jnp.zeros((mid, HEAD), F32)
        for r in range(0, HEADS_LOCAL * rows, wide):
            tile(k_in.at[slot], v_in.at[slot], sums, k0, mid, r, wide, False)

    hand_on(0)
    arrived(1, 0)
    half_block(1, 0)
    hand_on(1)
    scatter_start(0, low_s, low_r, 0, 2 * HEAD)

    i = lax.broadcasted_iota(jnp.int32, (1, rows), 1)
    set_thr(jnp.maximum(first_allowed(seg_in[0], c >= REACH), i + 1))
    for h in range(HEADS_LOCAL):
        for r in range(0, rows, edge):
            tile(
                k_in.at[0], v_in.at[0], acc.at[0], r, rows - r, h * rows + r, edge, False
            )

    scales = (1.0, SCORE_SCALE)

    def send_last(part):
        span = slice(part * mid, (part + 1) * mid)
        for which in range(2):
            part_out[3, which, span] = (scales[which] * acc[1, which, span]).astype(BF16)
            part_copy(3, which, cross_core, part).start()

    def send_across(part, which):
        span = slice(part * mid, (part + 1) * mid)
        part_copy(3, which, cross_core, part).wait()
        part_out[2, which, span] = (
            scales[which] * acc[2, which, span] + part_in[3, which, span].astype(F32)
        ).astype(BF16)
        part_copy(2, which, ctx_at(-2), part).start()

    def half_step(step, carry):
        @pl.when(step == 0)
        def _():
            arrived(1, 1)

        @pl.when(step == 1)
        def _():
            arrived(2, 0)
            for which in groups[0]:
                kv_copy(which, 3, cross_core, 2).start()

        @pl.when(step == 2)
        def _():
            arrived(2, 1)
            for which in groups[1]:
                kv_copy(which, 3, cross_core, 2).start()
            arrived(3, 0)

        @pl.when(step == 4)
        def _():
            arrived(3, 1)

        slot = jnp.where(step == 0, 1, 2 + (step + 1) % 2)
        part = jnp.where(step == 0, 1, (step - 1) // 2)
        half_block(slot, part)

        @pl.when(step == 0)
        def _():
            part_out[1, 0] = acc[1, 0].astype(BF16)
            part_copy(1, 0, cross_core).start()
            part_out[1, 1] = (SCORE_SCALE * acc[1, 1]).astype(BF16)
            part_copy(1, 1, cross_core).start()

            @pl.when(core == 0)
            def _():
                part_out[0, 0] = acc[0, 0].astype(BF16)
                part_copy(0, 0, ctx_at(-REACH)).start()
                part_out[0, 1] = (SCORE_SCALE * acc[0, 1]).astype(BF16)
                part_copy(0, 1, ctx_at(-REACH)).start()

        @pl.when(step == 1)
        def _():
            part_copy(1, 0, cross_core).wait()
            part_copy(1, 1, cross_core).wait()

            @pl.when(core == 1)
            def _():
                part_out[0, 0] = (acc[0, 0] + part_in[1, 0].astype(F32)).astype(BF16)
                part_copy(0, 0, ctx_at(-REACH)).start()
                part_out[0, 1] = (
                    SCORE_SCALE * acc[0, 1] + part_in[1, 1].astype(F32)
                ).astype(BF16)
                part_copy(0, 1, ctx_at(-REACH)).start()

        @pl.when(step == 2)
        def _():
            send_last(0)

        @pl.when(step == 3)
        def _():
            send_across(0, 0)
            scatter_finish(0, low_s, low_r, low_g, 0, 2 * HEAD)

        @pl.when(step == 4)
        def _():
            send_last(1)

        return carry

    lax.fori_loop(0, 5, half_step, 0)

    token_scale = 1.0 / math.sqrt(rows * n_ctx)

    dq_low[...] = (SCORE_SCALE * dq_acc[...]).astype(BF16)
    back_s[0:HEAD, :] = (
        contract(bq_ref[:, 0:HEAD], dq_low[:, 0:rows], 1, 0)
        + contract(bq_ref[:, HEAD : 2 * HEAD], dq_low[:, rows : 2 * rows], 1, 0)
    ).astype(BF16)
    scatter_start(2, back_s, back_r, 0, HEAD)
    send_across(1, 0)

    gather_finish(0, low_g, 0, 2 * HEAD)
    base = 2 * width
    for h in range(HEADS_LOCAL):
        g_all[base + h * HEAD : base + (h + 1) * HEAD, :] = token_scale * contract(
            dq_low[:, h * rows : (h + 1) * rows], low_g[0:HEAD, :], 1, 1
        )
    scatter_finish(2, back_s, back_r, back_g, 0, HEAD)

    def gathered(which):
        near = jnp.where(core == 0, part_in[1, which].astype(F32), 0.0)
        part_copy(0, which, ctx_at(-REACH)).wait()
        part_copy(2, which, ctx_at(-2), 0).wait()
        part_copy(2, which, ctx_at(-2), 1).wait()
        return near + part_in[0, which].astype(F32) + part_in[2, which].astype(F32)

    dv_low[...] = (own[0] + gathered(0)).astype(BF16)
    back_s[HEAD : 2 * HEAD, :] = contract(bv_ref[...], dv_low[...], 1, 1).astype(BF16)
    scatter_start(4, back_s, back_r, HEAD, HEAD)
    send_across(0, 1)
    send_across(1, 1)
    g_all[total - HEAD : total, :] = token_scale * contract(
        low_g[HEAD : 2 * HEAD, :], dv_low[...], 1, 0
    )
    gather_finish(2, back_g, 0, HEAD)
    g_all[0:width, :] = token_scale * contract(x_ref[...], back_g[0:HEAD, :], 1, 1)

    scatter_finish(4, back_s, back_r, back_g, HEAD, HEAD)
    gather_finish(4, back_g, HEAD, HEAD)
    g_all[width : 2 * width, :] = token_scale * contract(
        x_ref[...], back_g[HEAD : 2 * HEAD, :], 1, 1
    )

    other = 1 - core
    own_half = pl.ds(pl.multiple_of(core * half, 16), half)
    half_s[...] = g_all[pl.ds(pl.multiple_of(other * half, 16), half), :].astype(BF16)

    def to_other(which, src, dst):
        return pltpu.make_async_remote_copy(
            src_ref=src,
            dst_ref=dst,
            send_sem=half_send.at[which],
            recv_sem=half_recv.at[which],
            device_id={"ctx": c + other - core},
            device_id_type=MESH,
        )

    swap = to_other(0, half_s, half_r)
    swap.start()
    swap.wait()
    g_all[0:half, :] = g_all[own_half, :] + half_r[...].astype(F32)
    piece_s[...] = g_all[0:half, :].astype(BF16)

    def piece_copy(offset):
        to = lax.rem(pair + offset, pairs)
        return pltpu.make_async_remote_copy(
            src_ref=piece_s.at[pl.ds(pl.multiple_of(to * piece, 16), piece)],
            dst_ref=piece_r.at[offset],
            send_sem=piece_send.at[0, offset],
            recv_sem=piece_recv.at[0, offset],
            device_id={"ctx": 2 * to + core},
            device_id_type=MESH,
        )

    for offset in range(1, pairs):
        piece_copy(offset).start()
    summed = g_all[pl.ds(pl.multiple_of(pair * piece, 16), piece), :]
    for offset in range(1, pairs):
        piece_copy(offset).wait()
        summed = summed + piece_r[offset].astype(F32)
    own_piece = pl.ds(pl.multiple_of(core * half + pair * piece, 16), piece)
    g_out[own_piece, :] = summed.astype(BF16)

    def spread_copy(offset):
        to = lax.rem(pair + offset, pairs)
        return pltpu.make_async_remote_copy(
            src_ref=g_out.at[own_piece],
            dst_ref=g_out.at[own_piece],
            send_sem=piece_send.at[1, offset],
            recv_sem=piece_recv.at[1, offset],
            device_id={"ctx": 2 * to + core},
            device_id_type=MESH,
        )

    for offset in range(1, pairs):
        spread_copy(offset).start()
    for offset in range(1, pairs):
        spread_copy(offset).wait()
    swap = to_other(1, g_out.at[own_half], g_out.at[own_half])
    swap.start()
    swap.wait()

    sums_ref[...] = g_out[...]
    key_grad_ref[...] = (SCORE_SCALE * own[1] + gathered(1)).astype(BF16)
    for which in range(5):
        for slot in range(REACH):
            kv_copy(which, slot, cross_core).wait_send()


def finish(key_ref, sums_ref, key_grad_ref, ga_q_ref, gb_q_ref, ga_v_ref, gb_v_ref):
    key_grad_ref[...] = key_ref[...]
    width = ga_q_ref.shape[0]
    base = 2 * width
    ga_q_ref[...] = sums_ref[0:width, :].astype(F32)
    ga_v_ref[...] = sums_ref[width : 2 * width, :].astype(F32)
    for h in range(HEADS_LOCAL):
        gb_q_ref[:, h * HEAD : (h + 1) * HEAD] = (
            sums_ref[base + h * HEAD : base + (h + 1) * HEAD, :].astype(F32).T
        )
    gb_v_ref[...] = sums_ref[base + HEADS_LOCAL * HEAD :, :].astype(F32)


def per_device(x, q, k, v, do, o, lse, seg, aq, bq, av, bv):
    n_ctx, n_tp = lax.axis_size("ctx"), lax.axis_size("tp")
    rows, width = x.shape
    chunk = rows // n_tp
    total = 2 * width + 3 * HEAD
    half = total // 2
    pairs = n_ctx // 2
    piece = half // pairs
    dma = pltpu.SemaphoreType.DMA
    vmem = pltpu.VMEM
    scratch = [
        vmem((width, rows), BF16),
        vmem((rows, 2 * HEAD), BF16),
        vmem((rows, HEAD), BF16),
        vmem((rows, HEAD), BF16),
        vmem((rows, 2 * HEAD), BF16),
        vmem((rows, 2 * HEAD), BF16),
        vmem((2, rows), F32),
        vmem((1, rows), jnp.int32),
        vmem((width, HEAD), BF16),
        vmem((HEAD, 2 * HEAD), BF16),
        vmem((width, HEAD), BF16),
        vmem((HEAD, HEAD), BF16),
        dma((12,)),
        vmem((REACH, rows, HEAD), BF16),
        vmem((REACH, rows, HEAD), BF16),
        vmem((REACH, 1, rows), jnp.int32),
        vmem((2 * rows, HEAD), BF16),
        vmem((2 * rows, HEAD), BF16),
        vmem((1, 2 * rows), F32),
        vmem((1, 2 * rows), F32),
        vmem((1, 2 * rows), jnp.int32),
        vmem((3, 2, rows, HEAD), F32),
        vmem((2, rows, HEAD), F32),
        vmem((HEAD, 2 * rows), F32),
        vmem((HEAD, 2 * rows), BF16),
        vmem((rows, HEAD), BF16),
        vmem((REACH, 2, rows, HEAD), BF16),
        vmem((REACH, 2, rows, HEAD), BF16),
        vmem((2 * HEAD, rows), BF16),
        vmem((n_tp, 2 * HEAD, chunk), BF16),
        vmem((2 * HEAD, rows), BF16),
        vmem((2 * HEAD, rows), BF16),
        vmem((n_tp, 2 * HEAD, chunk), BF16),
        vmem((2 * HEAD, rows), BF16),
        vmem((total, HEAD), F32),
        vmem((half, HEAD), BF16),
        vmem((half, HEAD), BF16),
        vmem((half, HEAD), BF16),
        vmem((pairs, piece, HEAD), BF16),
        vmem((total, HEAD), BF16),
        dma((5, REACH)),
        dma((5, REACH)),
        dma((REACH, 4)),
        dma((REACH, 4)),
        dma((6, n_tp)),
        dma((6, n_tp)),
        dma((2,)),
        dma((2,)),
        dma((2, pairs)),
        dma((2, pairs)),
    ]
    whole = pl.BlockSpec(memory_space=pltpu.VMEM)
    flops = 10 * 9 * rows * rows * HEAD
    key_grad, sums = pl.pallas_call(
        functools.partial(kernel, n_ctx, n_tp),
        out_shape=[
            jax.ShapeDtypeStruct((rows, HEAD), BF16),
            jax.ShapeDtypeStruct((total, HEAD), BF16),
        ],
        in_specs=[pl.BlockSpec(memory_space=pl.ANY)] * 12,
        out_specs=[whole] * 2,
        scratch_shapes=scratch,
        compiler_params=pltpu.CompilerParams(
            collective_id=0, has_side_effects=True, vmem_limit_bytes=56 * 1024 * 1024
        ),
        cost_estimate=pl.CostEstimate(
            flops=flops, bytes_accessed=8 * 1024 * 1024, transcendentals=9 * rows * rows
        ),
    )(x.T, q, k, v, do, o, lse, seg.reshape(1, rows), aq, bq, av, bv)
    return pl.pallas_call(
        finish,
        out_shape=[
            jax.ShapeDtypeStruct((rows, HEAD), BF16),
            jax.ShapeDtypeStruct((width, HEAD), F32),
            jax.ShapeDtypeStruct((HEAD, 2 * HEAD), F32),
            jax.ShapeDtypeStruct((width, HEAD), F32),
            jax.ShapeDtypeStruct((HEAD, HEAD), F32),
        ],
        in_specs=[whole] * 2,
        out_specs=[whole] * 5,
    )(key_grad, sums)


def solution(mesh):
    placed = (
        P("ctx", "tp"),
        P("ctx", "tp"),
        P("ctx", "tp"),
        P("ctx", "tp"),
        P("ctx", "tp"),
        P("ctx", "tp"),
        P("tp", "ctx"),
        P("ctx"),
        P("tp", None),
        P(None, "tp"),
        P("tp", None),
        P(None, "tp"),
    )
    return jax.shard_map(
        per_device,
        mesh=mesh,
        in_specs=placed,
        out_specs=(P("ctx", "tp"), P("tp", None), P(None, "tp"), P("tp", None), P(None, "tp")),
        check_vma=False,
    )
```

```python
import functools
import math

import jax
import jax.numpy as jnp
from jax import lax
from jax.experimental import pallas as pl
from jax.experimental.pallas import tpu as pltpu
from jax.sharding import PartitionSpec as P

HEAD = 128
HEADS_LOCAL = 2
REACH = 4
SCORE_SCALE = 144.0 ** (-0.5)
LOG2E = 1.4426950408889634
BF16 = jnp.bfloat16
F32 = jnp.float32
MESH = pl.DeviceIdType.MESH


def contract(a, b, dim_a, dim_b):
    return lax.dot_general(
        a, b, (((dim_a,), (dim_b,)), ((), ())), preferred_element_type=F32
    )


def kernel(
    n_ctx,
    n_tp,
    x_hbm,
    q_hbm,
    k_hbm,
    v_hbm,
    do_hbm,
    o_hbm,
    lse_hbm,
    seg_hbm,
    aq_hbm,
    bq_hbm,
    av_hbm,
    bv_hbm,
    key_grad_ref,
    sums_ref,
    x_ref,
    q_ref,
    k_ref,
    v_ref,
    do_ref,
    o_ref,
    lse_ref,
    seg_ref,
    aq_ref,
    bq_ref,
    av_ref,
    bv_ref,
    load_sem,
    k_in,
    v_in,
    seg_in,
    q_st,
    do_st,
    lse_st,
    delta_st,
    thr_st,
    acc,
    own,
    dq_acc,
    dq_low,
    dv_low,
    part_out,
    part_in,
    low_s,
    low_r,
    low_g,
    back_s,
    back_r,
    back_g,
    g_all,
    half_s,
    half_r,
    piece_s,
    piece_r,
    g_out,
    kv_send,
    kv_recv,
    part_send,
    part_recv,
    tp_send,
    tp_recv,
    half_send,
    half_recv,
    piece_send,
    piece_recv,
):
    rows = k_ref.shape[0]
    width = x_ref.shape[0]
    chunk = rows // n_tp
    pairs = n_ctx // 2
    total = g_all.shape[0]
    half = total // 2
    piece = half // pairs
    c = lax.axis_index("ctx")
    t = lax.axis_index("tp")
    core = lax.rem(c, 2)
    pair = c // 2
    side = lax.rem(pair, 2)

    def ctx_at(offset):
        return lax.rem(c + (offset + n_ctx), n_ctx)

    def tp_at(offset):
        return lax.rem(t + offset, n_tp)

    barrier = pltpu.get_barrier_semaphore()
    offsets = {s % n_ctx for s in range(-REACH, REACH + 1)} | set(range(0, n_ctx, 2))
    offsets = sorted(offsets - {0})
    for offset in offsets:
        pl.semaphore_signal(
            barrier, inc=1, device_id={"ctx": ctx_at(offset)}, device_id_type=MESH
        )
    for offset in range(1, n_tp):
        pl.semaphore_signal(
            barrier, inc=1, device_id={"tp": tp_at(offset)}, device_id_type=MESH
        )
    loads = {}
    for place, (src, dst) in enumerate(
        (
            (k_hbm, k_ref),
            (v_hbm, v_ref),
            (seg_hbm, seg_ref),
            (aq_hbm, aq_ref),
            (av_hbm, av_ref),
            (x_hbm, x_ref),
            (q_hbm, q_ref),
            (do_hbm, do_ref),
            (o_hbm, o_ref),
            (lse_hbm, lse_ref),
            (bq_hbm, bq_ref),
            (bv_hbm, bv_ref),
        )
    ):
        loads[place] = pltpu.make_async_copy(src, dst, load_sem.at[place])
        loads[place].start()
    for place in range(6):
        loads[place].wait()
    low_s[0:HEAD, :] = contract(aq_ref[...], x_ref[...], 0, 0).astype(BF16)
    low_s[HEAD : 2 * HEAD, :] = contract(av_ref[...], x_ref[...], 0, 0).astype(BF16)
    pl.semaphore_wait(barrier, len(offsets) + n_tp - 1)

    cross_core = c + 1 - 2 * core
    cross_x = c + 2 - 4 * side
    mid = rows // 2
    pieces = ((seg_ref, seg_in, None), (k_ref, k_in, 0), (v_ref, v_in, 0), (k_ref, k_in, 1), (v_ref, v_in, 1))
    groups = ((0, 1, 2), (3, 4))

    def kv_copy(which, slot, target, relay=None):
        src, dst, part = pieces[which]
        src = src if relay is None else dst.at[relay]
        dst = dst.at[slot]
        if part is not None:
            src, dst = src.at[pl.ds(part * mid, mid)], dst.at[pl.ds(part * mid, mid)]
        return pltpu.make_async_remote_copy(
            src_ref=src,
            dst_ref=dst,
            send_sem=kv_send.at[which, slot],
            recv_sem=kv_recv.at[which, slot],
            device_id={"ctx": target},
            device_id_type=MESH,
        )

    def arrived(slot, part):
        for which in groups[part]:
            kv_copy(which, slot, cross_core).wait_recv()

    for which in range(5):
        kv_copy(which, 0, ctx_at(REACH)).start()

        @pl.when(core == 0)
        def _(which=which):
            kv_copy(which, 1, cross_core).start()

        @pl.when(side == 0)
        def _(which=which):
            kv_copy(which, 2, cross_x).start()

    def hand_on(part):
        for which in groups[part]:
            kv_copy(which, 0, cross_core).wait_recv()

            @pl.when(core == 1)
            def _(which=which):
                kv_copy(which, 1, cross_core, 0).start()

            @pl.when(side == 1)
            def _(which=which):
                kv_copy(which, 2, cross_x, 0).start()

    def part_copy(slot, which, target, part=None):
        src, dst = part_out.at[slot, which], part_in.at[slot, which]
        place = 2 * which
        if part is not None:
            src, dst = src.at[pl.ds(part * mid, mid)], dst.at[pl.ds(part * mid, mid)]
            place = place + part
        return pltpu.make_async_remote_copy(
            src_ref=src,
            dst_ref=dst,
            send_sem=part_send.at[slot, place],
            recv_sem=part_recv.at[slot, place],
            device_id={"ctx": target},
            device_id_type=MESH,
        )

    def scatter_copy(which, src, dst, first, high, offset):
        to = tp_at(offset)
        return pltpu.make_async_remote_copy(
            src_ref=src.at[pl.ds(first, high), pl.ds(pl.multiple_of(to * chunk, chunk), chunk)],
            dst_ref=dst.at[offset, pl.ds(first, high)],
            send_sem=tp_send.at[which, offset],
            recv_sem=tp_recv.at[which, offset],
            device_id={"tp": to},
            device_id_type=MESH,
        )

    mine = pl.ds(pl.multiple_of(t * chunk, chunk), chunk)

    def gather_copy(which, ref, first, high, offset):
        place = ref.at[pl.ds(first, high), mine]
        return pltpu.make_async_remote_copy(
            src_ref=place,
            dst_ref=place,
            send_sem=tp_send.at[which, offset],
            recv_sem=tp_recv.at[which, offset],
            device_id={"tp": tp_at(offset)},
            device_id_type=MESH,
        )

    def scatter_start(which, src, dst, first, high):
        for offset in range(1, n_tp):
            scatter_copy(which, src, dst, first, high, offset).start()

    def scatter_finish(which, src, dst, ref, first, high):
        for offset in range(1, n_tp):
            scatter_copy(which, src, dst, first, high, offset).wait()
        part = src[first : first + high, mine].astype(F32)
        for offset in range(1, n_tp):
            part = part + dst[offset, first : first + high, :].astype(F32)
        ref[first : first + high, mine] = part.astype(BF16)
        for offset in range(1, n_tp):
            gather_copy(which + 1, ref, first, high, offset).start()

    def gather_finish(which, ref, first, high):
        for offset in range(1, n_tp):
            gather_copy(which + 1, ref, first, high, offset).wait()

    for place in range(6, 12):
        loads[place].wait()

    ones = jnp.ones((8, HEAD), BF16)
    for h in range(HEADS_LOCAL):
        cols = slice(h * HEAD, (h + 1) * HEAD)
        span = slice(h * rows, (h + 1) * rows)
        q_st[span, :] = q_ref[:, cols]
        grad = do_ref[:, cols]
        do_st[span, :] = grad
        prod = grad.astype(F32) * o_ref[:, cols].astype(F32)
        high = prod.astype(BF16)
        rest = (prod - high.astype(F32)).astype(BF16)
        delta = contract(ones, high, 1, 1) + contract(ones, rest, 1, 1)
        delta_st[:, span] = delta[0:1, :]
        lse_st[:, span] = lse_ref[h : h + 1, :] * LOG2E

    def first_allowed(block, present):
        ids = seg_ref[...]
        found = jnp.zeros((1, rows), jnp.int32)
        for doc in range(1, 4):
            below = jnp.sum((block < doc).astype(F32), axis=1, keepdims=True)
            found = jnp.where(ids == doc, below.astype(jnp.int32), found)
        return jnp.where(present, found, rows)

    def set_thr(found):
        for h in range(HEADS_LOCAL):
            thr_st[:, h * rows : (h + 1) * rows] = found

    def tile(keys, values, sums, k0, kt, r0, rt, causal):
        ks, rs = pl.ds(k0, kt), pl.ds(r0, rt)
        key, value = keys[ks, :], values[ks, :]
        query, grad = q_st[rs, :], do_st[rs, :]
        j = lax.broadcasted_iota(jnp.int32, (kt, rt), 0) + k0
        mask = j >= thr_st[:, rs]
        if causal:
            i = lax.broadcasted_iota(jnp.int32, (1, rt), 1) + (r0 % rows)
            mask = mask & (j <= i)
        score = contract(key, query, 1, 1)
        dprob = contract(value, grad, 1, 1)
        prob = jnp.where(mask, jnp.exp2(score * (SCORE_SCALE * LOG2E) - lse_st[:, rs]), 0.0)
        dscore = (prob * (dprob - delta_st[:, rs])).astype(BF16)
        sums[0, ks, :] += contract(prob.astype(BF16), grad, 1, 0)
        sums[1, ks, :] += contract(dscore, query, 1, 0)
        dq_acc[:, rs] += contract(key, dscore, 0, 0)

    edge = min(256, rows)
    wide = min(512, rows)

    dq_acc[...] = jnp.zeros_like(dq_acc)
    own[...] = jnp.zeros_like(own)
    acc[0] = jnp.zeros_like(own)
    set_thr(first_allowed(seg_ref[...], True))
    for h in range(HEADS_LOCAL):
        for r in range(0, rows, edge):
            if r:
                tile(k_ref, v_ref, own, 0, r, h * rows + r, edge, False)
            tile(k_ref, v_ref, own, r, edge, h * rows + r, edge, True)

    def half_block(slot, part):
        back = jnp.where(slot == 2, 2, jnp.where((slot == 1) == (core == 1), 1, 3))
        set_thr(first_allowed(seg_in[slot], c >= back))
        k0 = pl.multiple_of(part * mid, mid)
        sums = acc.at[2 - slot % 2]
        for which in range(2):
            sums[which, pl.ds(k0, mid), :] = jnp.zeros((mid, HEAD), F32)
        for r in range(0, HEADS_LOCAL * rows, wide):
            tile(k_in.at[slot], v_in.at[slot], sums, k0, mid, r, wide, False)

    hand_on(0)
    arrived(1, 0)
    half_block(1, 0)
    hand_on(1)
    scatter_start(0, low_s, low_r, 0, 2 * HEAD)

    i = lax.broadcasted_iota(jnp.int32, (1, rows), 1)
    set_thr(jnp.maximum(first_allowed(seg_in[0], c >= REACH), i + 1))
    for h in range(HEADS_LOCAL):
        for r in range(0, rows, edge):
            tile(
                k_in.at[0], v_in.at[0], acc.at[0], r, rows - r, h * rows + r, edge, False
            )

    scales = (1.0, SCORE_SCALE)

    def send_last(part):
        span = slice(part * mid, (part + 1) * mid)
        for which in range(2):
            part_out[3, which, span] = (scales[which] * acc[1, which, span]).astype(BF16)
            part_copy(3, which, cross_core, part).start()

    def send_across(part, which):
        span = slice(part * mid, (part + 1) * mid)
        part_copy(3, which, cross_core, part).wait()
        part_out[2, which, span] = (
            scales[which] * acc[2, which, span] + part_in[3, which, span].astype(F32)
        ).astype(BF16)
        part_copy(2, which, ctx_at(-2), part).start()

    def half_step(step, carry):
        @pl.when(step == 0)
        def _():
            arrived(1, 1)

        @pl.when(step == 1)
        def _():
            arrived(2, 0)
            for which in groups[0]:
                kv_copy(which, 3, cross_core, 2).start()

        @pl.when(step == 2)
        def _():
            arrived(2, 1)
            for which in groups[1]:
                kv_copy(which, 3, cross_core, 2).start()
            arrived(3, 0)

        @pl.when(step == 4)
        def _():
            arrived(3, 1)

        slot = jnp.where(step == 0, 1, 2 + (step + 1) % 2)
        part = jnp.where(step == 0, 1, (step - 1) // 2)
        half_block(slot, part)

        @pl.when(step == 0)
        def _():
            part_out[1, 0] = acc[1, 0].astype(BF16)
            part_copy(1, 0, cross_core).start()
            part_out[1, 1] = (SCORE_SCALE * acc[1, 1]).astype(BF16)
            part_copy(1, 1, cross_core).start()

            @pl.when(core == 0)
            def _():
                part_out[0, 0] = acc[0, 0].astype(BF16)
                part_copy(0, 0, ctx_at(-REACH)).start()
                part_out[0, 1] = (SCORE_SCALE * acc[0, 1]).astype(BF16)
                part_copy(0, 1, ctx_at(-REACH)).start()

        @pl.when(step == 1)
        def _():
            part_copy(1, 0, cross_core).wait()
            part_copy(1, 1, cross_core).wait()

            @pl.when(core == 1)
            def _():
                part_out[0, 0] = (acc[0, 0] + part_in[1, 0].astype(F32)).astype(BF16)
                part_copy(0, 0, ctx_at(-REACH)).start()
                part_out[0, 1] = (
                    SCORE_SCALE * acc[0, 1] + part_in[1, 1].astype(F32)
                ).astype(BF16)
                part_copy(0, 1, ctx_at(-REACH)).start()

        @pl.when(step == 2)
        def _():
            send_last(0)

        @pl.when(step == 3)
        def _():
            send_across(0, 0)
            scatter_finish(0, low_s, low_r, low_g, 0, 2 * HEAD)

        @pl.when(step == 4)
        def _():
            send_last(1)

        return carry

    lax.fori_loop(0, 5, half_step, 0)

    token_scale = 1.0 / math.sqrt(rows * n_ctx)

    dq_low[...] = (SCORE_SCALE * dq_acc[...]).astype(BF16)
    back_s[0:HEAD, :] = (
        contract(bq_ref[:, 0:HEAD], dq_low[:, 0:rows], 1, 0)
        + contract(bq_ref[:, HEAD : 2 * HEAD], dq_low[:, rows : 2 * rows], 1, 0)
    ).astype(BF16)
    scatter_start(2, back_s, back_r, 0, HEAD)
    send_across(1, 0)

    gather_finish(0, low_g, 0, 2 * HEAD)
    base = 2 * width
    for h in range(HEADS_LOCAL):
        g_all[base + h * HEAD : base + (h + 1) * HEAD, :] = token_scale * contract(
            dq_low[:, h * rows : (h + 1) * rows], low_g[0:HEAD, :], 1, 1
        )
    scatter_finish(2, back_s, back_r, back_g, 0, HEAD)

    def gathered(which):
        near = jnp.where(core == 0, part_in[1, which].astype(F32), 0.0)
        part_copy(0, which, ctx_at(-REACH)).wait()
        part_copy(2, which, ctx_at(-2), 0).wait()
        part_copy(2, which, ctx_at(-2), 1).wait()
        return near + part_in[0, which].astype(F32) + part_in[2, which].astype(F32)

    dv_low[...] = (own[0] + gathered(0)).astype(BF16)
    back_s[HEAD : 2 * HEAD, :] = contract(bv_ref[...], dv_low[...], 1, 1).astype(BF16)
    scatter_start(4, back_s, back_r, HEAD, HEAD)
    send_across(0, 1)
    send_across(1, 1)
    g_all[total - HEAD : total, :] = token_scale * contract(
        low_g[HEAD : 2 * HEAD, :], dv_low[...], 1, 0
    )
    gather_finish(2, back_g, 0, HEAD)
    g_all[0:width, :] = token_scale * contract(x_ref[...], back_g[0:HEAD, :], 1, 1)

    scatter_finish(4, back_s, back_r, back_g, HEAD, HEAD)
    gather_finish(4, back_g, HEAD, HEAD)
    g_all[width : 2 * width, :] = token_scale * contract(
        x_ref[...], back_g[HEAD : 2 * HEAD, :], 1, 1
    )

    other = 1 - core
    own_half = pl.ds(pl.multiple_of(core * half, 16), half)
    half_s[...] = g_all[pl.ds(pl.multiple_of(other * half, 16), half), :].astype(BF16)

    def to_other(which, src, dst):
        return pltpu.make_async_remote_copy(
            src_ref=src,
            dst_ref=dst,
            send_sem=half_send.at[which],
            recv_sem=half_recv.at[which],
            device_id={"ctx": c + other - core},
            device_id_type=MESH,
        )

    swap = to_other(0, half_s, half_r)
    swap.start()
    swap.wait()
    g_all[0:half, :] = g_all[own_half, :] + half_r[...].astype(F32)
    piece_s[...] = g_all[0:half, :].astype(BF16)

    def piece_copy(offset):
        to = lax.rem(pair + offset, pairs)
        return pltpu.make_async_remote_copy(
            src_ref=piece_s.at[pl.ds(pl.multiple_of(to * piece, 16), piece)],
            dst_ref=piece_r.at[offset],
            send_sem=piece_send.at[0, offset],
            recv_sem=piece_recv.at[0, offset],
            device_id={"ctx": 2 * to + core},
            device_id_type=MESH,
        )

    far_first = sorted(range(1, pairs), key=lambda offset: abs(2 * offset - pairs))
    for offset in far_first:
        piece_copy(offset).start()
    summed = g_all[pl.ds(pl.multiple_of(pair * piece, 16), piece), :]
    for offset in range(1, pairs):
        piece_copy(offset).wait()
        summed = summed + piece_r[offset].astype(F32)
    own_piece = pl.ds(pl.multiple_of(core * half + pair * piece, 16), piece)
    g_out[own_piece, :] = summed.astype(BF16)

    def spread_copy(offset):
        to = lax.rem(pair + offset, pairs)
        return pltpu.make_async_remote_copy(
            src_ref=g_out.at[own_piece],
            dst_ref=g_out.at[own_piece],
            send_sem=piece_send.at[1, offset],
            recv_sem=piece_recv.at[1, offset],
            device_id={"ctx": 2 * to + core},
            device_id_type=MESH,
        )

    for offset in far_first:
        spread_copy(offset).start()
    for offset in range(1, pairs):
        spread_copy(offset).wait()
    swap = to_other(1, g_out.at[own_half], g_out.at[own_half])
    swap.start()
    swap.wait()

    sums_ref[...] = g_out[...]
    key_grad_ref[...] = (SCORE_SCALE * own[1] + gathered(1)).astype(BF16)
    for which in range(5):
        for slot in range(REACH):
            kv_copy(which, slot, cross_core).wait_send()


def finish(key_ref, sums_ref, key_grad_ref, ga_q_ref, gb_q_ref, ga_v_ref, gb_v_ref):
    key_grad_ref[...] = key_ref[...]
    width = ga_q_ref.shape[0]
    base = 2 * width
    ga_q_ref[...] = sums_ref[0:width, :].astype(F32)
    ga_v_ref[...] = sums_ref[width : 2 * width, :].astype(F32)
    for h in range(HEADS_LOCAL):
        gb_q_ref[:, h * HEAD : (h + 1) * HEAD] = (
            sums_ref[base + h * HEAD : base + (h + 1) * HEAD, :].astype(F32).T
        )
    gb_v_ref[...] = sums_ref[base + HEADS_LOCAL * HEAD :, :].astype(F32)


def per_device(x, q, k, v, do, o, lse, seg, aq, bq, av, bv):
    n_ctx, n_tp = lax.axis_size("ctx"), lax.axis_size("tp")
    rows, width = x.shape
    chunk = rows // n_tp
    total = 2 * width + 3 * HEAD
    half = total // 2
    pairs = n_ctx // 2
    piece = half // pairs
    dma = pltpu.SemaphoreType.DMA
    vmem = pltpu.VMEM
    scratch = [
        vmem((width, rows), BF16),
        vmem((rows, 2 * HEAD), BF16),
        vmem((rows, HEAD), BF16),
        vmem((rows, HEAD), BF16),
        vmem((rows, 2 * HEAD), BF16),
        vmem((rows, 2 * HEAD), BF16),
        vmem((2, rows), F32),
        vmem((1, rows), jnp.int32),
        vmem((width, HEAD), BF16),
        vmem((HEAD, 2 * HEAD), BF16),
        vmem((width, HEAD), BF16),
        vmem((HEAD, HEAD), BF16),
        dma((12,)),
        vmem((REACH, rows, HEAD), BF16),
        vmem((REACH, rows, HEAD), BF16),
        vmem((REACH, 1, rows), jnp.int32),
        vmem((2 * rows, HEAD), BF16),
        vmem((2 * rows, HEAD), BF16),
        vmem((1, 2 * rows), F32),
        vmem((1, 2 * rows), F32),
        vmem((1, 2 * rows), jnp.int32),
        vmem((3, 2, rows, HEAD), F32),
        vmem((2, rows, HEAD), F32),
        vmem((HEAD, 2 * rows), F32),
        vmem((HEAD, 2 * rows), BF16),
        vmem((rows, HEAD), BF16),
        vmem((REACH, 2, rows, HEAD), BF16),
        vmem((REACH, 2, rows, HEAD), BF16),
        vmem((2 * HEAD, rows), BF16),
        vmem((n_tp, 2 * HEAD, chunk), BF16),
        vmem((2 * HEAD, rows), BF16),
        vmem((2 * HEAD, rows), BF16),
        vmem((n_tp, 2 * HEAD, chunk), BF16),
        vmem((2 * HEAD, rows), BF16),
        vmem((total, HEAD), F32),
        vmem((half, HEAD), BF16),
        vmem((half, HEAD), BF16),
        vmem((half, HEAD), BF16),
        vmem((pairs, piece, HEAD), BF16),
        vmem((total, HEAD), BF16),
        dma((5, REACH)),
        dma((5, REACH)),
        dma((REACH, 4)),
        dma((REACH, 4)),
        dma((6, n_tp)),
        dma((6, n_tp)),
        dma((2,)),
        dma((2,)),
        dma((2, pairs)),
        dma((2, pairs)),
    ]
    whole = pl.BlockSpec(memory_space=pltpu.VMEM)
    flops = 10 * 9 * rows * rows * HEAD
    key_grad, sums = pl.pallas_call(
        functools.partial(kernel, n_ctx, n_tp),
        out_shape=[
            jax.ShapeDtypeStruct((rows, HEAD), BF16),
            jax.ShapeDtypeStruct((total, HEAD), BF16),
        ],
        in_specs=[pl.BlockSpec(memory_space=pl.ANY)] * 12,
        out_specs=[whole] * 2,
        scratch_shapes=scratch,
        compiler_params=pltpu.CompilerParams(
            collective_id=0, has_side_effects=True, vmem_limit_bytes=56 * 1024 * 1024
        ),
        cost_estimate=pl.CostEstimate(
            flops=flops, bytes_accessed=8 * 1024 * 1024, transcendentals=9 * rows * rows
        ),
    )(x.T, q, k, v, do, o, lse, seg.reshape(1, rows), aq, bq, av, bv)
    return pl.pallas_call(
        finish,
        out_shape=[
            jax.ShapeDtypeStruct((rows, HEAD), BF16),
            jax.ShapeDtypeStruct((width, HEAD), F32),
            jax.ShapeDtypeStruct((HEAD, 2 * HEAD), F32),
            jax.ShapeDtypeStruct((width, HEAD), F32),
            jax.ShapeDtypeStruct((HEAD, HEAD), F32),
        ],
        in_specs=[whole] * 2,
        out_specs=[whole] * 5,
    )(key_grad, sums)


def solution(mesh):
    placed = (
        P("ctx", "tp"),
        P("ctx", "tp"),
        P("ctx", "tp"),
        P("ctx", "tp"),
        P("ctx", "tp"),
        P("ctx", "tp"),
        P("tp", "ctx"),
        P("ctx"),
        P("tp", None),
        P(None, "tp"),
        P("tp", None),
        P(None, "tp"),
    )
    return jax.shard_map(
        per_device,
        mesh=mesh,
        in_specs=placed,
        out_specs=(P("ctx", "tp"), P("tp", None), P(None, "tp"), P("tp", None), P(None, "tp")),
        check_vma=False,
    )
```
